512 devices in a mesh: dp: 16 (over z, core), seq: 32 (over y, x).
Axes of the slice: x: 4, y: 8, z: 8, core: 2. Of those that a mesh axis runs over, the one named last changes fastest.
Arguments:
- features: bfloat16 [16, 32, 128, 2560], P('dp', None, 'seq'), may hold values from -6 to 6
- frozen_query_weight: bfloat16 [16, 32, 128, 4096], P('dp', None, 'seq'), may hold values from -100 to 100
- source_keys: bfloat16 [16, 32, 128, 4096], P('dp', None, 'seq'), may hold values from -6 to 6
- source_values: bfloat16 [16, 32, 128, 4096], P('dp', None, 'seq'), may hold values from -6 to 6
- output_gradient: bfloat16 [16, 32, 128, 4096], P('dp', None, 'seq'), may hold values from -6 to 6
- adapter_down_weight: bfloat16 [2560, 64], replicated, may hold values from -0.125 to 0.125
- adapter_up_weight: bfloat16 [64, 4096], replicated, may hold values from -0.75 to 0.75
- source_block_plan: int32 [16, 32], replicated, may hold values from 0 to 511, as said below
- segments: int32 [16, 4096], P('dp'), may hold values from 0 to 1, never falling along the last dimension, each value on 1 to 2560 neighbouring positions
Outputs:
- down_grad: float32 [2560, 64], P('seq')
- up_grad: float32 [64, 4096], P(None, 'seq')
- log_norm: float32 [16, 32, 4096], P('dp', 'seq')
The draws below stay inside these ranges and needn't reach their ends.
Inputs may be any that keep to these rules, and one draw needn't show every extreme that they name: `source_block_plan`: each entry names a source block as group * 32 + block; every source block is named exactly once; from one group to another group at most 2 blocks go, and some pairs of groups carry exactly 2. Within a group the segment numbers never fall and all 2 segments occur; a segment spans at most 2560 positions.
All inputs are finite; a program needn't handle non-finite values.
Results may differ from the reference program's by a relative error of at most 0.0087.
Values may be sent and summed in bfloat16 or wider, within the bound.
A program may use at most 64 MiB of HBM per device.

```python
import math
import jax
import jax.numpy as jnp
import numpy as np
from jax import lax

INPUT_FEATURES = 2560
HEAD_SIZE = 128
ADAPTER_RANK = 64
BLOCK = 128
CAP = 2
CLIPS = 2
HEAD_TOTAL = 32
GROUPS = 16
BLOCKS = 32
LENGTH = 4096
SEG_MOST = 2560
SHIFTS = 8


def shared_keys(key):
    return jnp.clip(jax.random.normal(key, (GROUPS * BLOCKS * BLOCK, HEAD_TOTAL * HEAD_SIZE), jnp.float32), -5.0, 5.0)


def draw_source_keys(key, part):
    common = shared_keys(key)
    return common.reshape(GROUPS, BLOCKS, BLOCK, HEAD_TOTAL * HEAD_SIZE).astype(jnp.bfloat16)


def draw_frozen_query_weight(key, part):
    common = shared_keys(key)
    key = jax.random.fold_in(key, 7)
    result = jnp.clip(jax.random.normal(key, common.shape, jnp.float32), -5.0, 5.0)
    return result.reshape(GROUPS, BLOCKS, BLOCK, HEAD_TOTAL * HEAD_SIZE).astype(jnp.bfloat16)


def draw_source_block_plan(key, part):
    key = jax.random.fold_in(key, 5)
    key_shift, key_order = jax.random.split(key)
    shifts = jax.random.permutation(key_shift, GROUPS - 1)[:SHIFTS] + 1
    orders = jax.vmap(lambda subkey: jax.random.permutation(subkey, BLOCKS))(jax.random.split(key_order, GROUPS))
    moved = orders[:, :SHIFTS * CAP].reshape(GROUPS, SHIFTS, CAP)
    group_ids = jnp.arange(GROUPS, dtype=jnp.int32)
    source_group = (group_ids[:, None] - shifts[None, :]) % GROUPS
    source_block = moved[source_group, jnp.arange(SHIFTS)[None, :], :]
    plan = group_ids[:, None] * BLOCKS + jnp.arange(BLOCKS, dtype=jnp.int32)[None, :]
    row_ids = jnp.broadcast_to(group_ids[:, None, None], moved.shape)
    entries = source_group[:, :, None] * BLOCKS + source_block
    return plan.at[row_ids, moved].set(entries).astype(jnp.int32)


def level_of(key, shape, pieces, smallest, largest):
    def one(dim, blocks):
        heights = jax.random.uniform(jax.random.fold_in(jax.random.fold_in(key, 6), dim), (blocks,), jnp.float32, smallest / len(pieces), largest / len(pieces))
        return jnp.repeat(jnp.exp(heights), shape[dim] // blocks).reshape((-1,) + (1,) * (len(shape) - dim - 1))

    loudness = one(*pieces[0])
    for cut in pieces[1:]:
        loudness = loudness * one(*cut)
    return loudness


def profile(amount, total, limit, skew):
    loads = [(1 << 20) // math.isqrt(grade ** skew) + 1 for grade in range(2, amount + 1)]
    spare, given = total - limit - (amount - 1), [1] * (amount - 1)
    while spare > 0:
        candidates = [i for i in range(amount - 1) if given[i] < limit]
        mass, left = sum([loads[i] for i in candidates]), spare
        for i in candidates:
            addition = min(limit - given[i], max(1, left * loads[i] // mass), spare)
            given[i] = given[i] + addition
            spare = spare - addition
    return np.array([limit] + given)


def ragged_sizes(key, count, total, reach, lean):
    if count == 2:
        one = jax.random.randint(key, (), max(1, total - reach), min(reach, total - 1) + 1)
        return jnp.stack([one, total - one])
    sizes = jnp.asarray(profile(count, total, reach, lean), jnp.int32)
    pairs = (count - 1) // 2
    source_of, receiver = sizes[1:1 + 2 * pairs:2], sizes[2:2 + 2 * pairs:2]
    room = jnp.minimum(source_of - 1, reach - receiver)
    passed = jax.random.randint(jax.random.fold_in(key, 1), (pairs,), 0, 1 << 20) % (room + 1)
    sizes = sizes.at[1:1 + 2 * pairs:2].set(source_of - passed).at[2:2 + 2 * pairs:2].set(receiver + passed)
    return sizes[jax.random.permutation(jax.random.fold_in(key, 2), count)]


def gaussian(stream_key, shape, scale, limit, cuts=(), kind=jnp.bfloat16):
    drawn = jax.random.normal(stream_key, shape, jnp.float32) * scale
    if len(cuts) > 0:
        drawn = level_of(stream_key, shape, cuts, -0.22, 0.18) * drawn
    return jnp.clip(drawn, min=-limit, max=limit).astype(kind)


def setup_inputs(seed: int = 0) -> dict:
    keys = jax.random.split(jax.random.key(seed), 10)
    features = gaussian(keys[0], (GROUPS, BLOCKS, BLOCK, INPUT_FEATURES), 1.0, 6.0, ((0, 16), (2, 32)))
    frozen_query_weight = draw_frozen_query_weight(jax.random.fold_in(keys[9], 71), 0)
    source_keys = draw_source_keys(jax.random.fold_in(keys[9], 71), 0)
    source_values = gaussian(keys[3], (GROUPS, BLOCKS, BLOCK, HEAD_TOTAL * HEAD_SIZE), 1.0, 6.0, ((0, 16), (2, 32)))
    output_gradient = gaussian(keys[4], (GROUPS, BLOCKS, BLOCK, HEAD_TOTAL * HEAD_SIZE), 1.0, 6.0, ((0, 16), (2, 32)))
    adapter_down_weight = gaussian(keys[5], (INPUT_FEATURES, ADAPTER_RANK), INPUT_FEATURES ** -0.5, 0.125)
    adapter_up_weight = gaussian(keys[6], (ADAPTER_RANK, HEAD_TOTAL * HEAD_SIZE), ADAPTER_RANK ** -0.5, 0.75)
    source_block_plan = draw_source_block_plan(jax.random.fold_in(keys[9], 71), 0)
    segments = jax.vmap(lambda own: jnp.searchsorted(jnp.cumsum(ragged_sizes(own, CLIPS, LENGTH, SEG_MOST, 1)), jnp.arange(LENGTH), side="right"))(jax.random.split(keys[8], GROUPS)).reshape((GROUPS, LENGTH)).astype(jnp.int32)
    return {"features": features, "frozen_query_weight": frozen_query_weight, "source_keys": source_keys, "source_values": source_values, "output_gradient": output_gradient, "adapter_down_weight": adapter_down_weight, "adapter_up_weight": adapter_up_weight, "source_block_plan": source_block_plan, "segments": segments}


def attend_head(query, key_rows, value_rows, cotangent, segment, clip_count, reach_rows):
    length = query.shape[0]
    width = query.shape[1]
    piece_count = 8
    piece_rows = reach_rows // piece_count
    scaling = 1.0 / math.sqrt(width)
    query_padded = jnp.pad(query, ((0, reach_rows), (0, 0)))
    grad_padded = jnp.pad(cotangent, ((0, reach_rows), (0, 0)))
    keys_padded = jnp.pad(key_rows, ((0, reach_rows), (0, 0)))
    values_padded = jnp.pad(value_rows, ((0, reach_rows), (0, 0)))
    segment_padded = jnp.pad(segment, (0, reach_rows), constant_values=-1)
    clip_ids = jnp.arange(clip_count, dtype=jnp.int32)
    starts = lax.optimization_barrier(jnp.sum((segment[None, :] < clip_ids[:, None]).astype(jnp.int32), axis=1)).astype(jnp.int32)

    def piece_pass(piece_index):
        clip_slice = piece_index // piece_count
        start = lax.dynamic_index_in_dim(starts, clip_slice, 0, keepdims=False).astype(jnp.int32)
        query_start = (start + piece_index % piece_count * piece_rows).astype(jnp.int32)
        query_tile = lax.dynamic_slice_in_dim(query_padded, query_start, piece_rows, 0)
        grad_tile = lax.dynamic_slice_in_dim(grad_padded, query_start, piece_rows, 0)
        seg_tile = lax.dynamic_slice_in_dim(segment_padded, query_start, piece_rows, 0)
        key_tile = lax.dynamic_slice_in_dim(keys_padded, start, reach_rows, 0)
        value_tile = lax.dynamic_slice_in_dim(values_padded, start, reach_rows, 0)
        seg_cols = lax.dynamic_slice_in_dim(segment_padded, start, reach_rows, 0)
        in_clip = seg_tile == clip_slice
        allowed = in_clip[:, None] & (seg_cols == clip_slice)[None, :]
        scores = lax.dot_general(query_tile, key_tile, (((1,), (1,)), ((), ())), preferred_element_type=jnp.float32) * scaling
        scores = jnp.where(allowed, scores, -1e+30)
        maximum = lax.optimization_barrier(jnp.max(scores, axis=1, keepdims=True))
        exponent = jnp.where(allowed, jnp.exp(scores - maximum), 0.0)
        totals = jnp.where(in_clip[:, None], lax.optimization_barrier(jnp.sum(exponent, axis=1, keepdims=True)), 1.0)
        log_norm = jnp.where(in_clip, maximum[:, 0] + jnp.log(totals[:, 0]), 0.0)
        probs = exponent / totals
        weights = probs.astype(jnp.bfloat16)
        attended = jnp.dot(weights, value_tile, preferred_element_type=jnp.float32)
        delta = lax.optimization_barrier(jnp.sum(grad_tile.astype(jnp.float32) * attended, axis=1, keepdims=True))
        dprob = lax.dot_general(grad_tile, value_tile, (((1,), (1,)), ((), ())), preferred_element_type=jnp.float32)
        dscore = (probs * (dprob - delta)).astype(jnp.bfloat16)
        query_gradient = (jnp.dot(dscore, key_tile, preferred_element_type=jnp.float32) * scaling).astype(jnp.bfloat16)
        query_gradient = jnp.where(in_clip[:, None], query_gradient, jnp.zeros((), jnp.bfloat16))
        return (query_gradient, log_norm, query_start)
    total_pieces = piece_count * (clip_count - 1)
    dquery_pieces, log_pieces, piece_starts = lax.map(piece_pass, jnp.arange(total_pieces, dtype=jnp.int32))

    def place(index, carry):
        grad_total, log_total = carry
        where_at = lax.dynamic_index_in_dim(piece_starts, index, 0, keepdims=False).astype(jnp.int32)
        grad_piece = lax.dynamic_index_in_dim(dquery_pieces, index, 0, keepdims=False)
        log_piece = lax.dynamic_index_in_dim(log_pieces, index, 0, keepdims=False)
        grad_old = lax.dynamic_slice_in_dim(grad_total, where_at, piece_rows, 0)
        log_old = lax.dynamic_slice_in_dim(log_total, where_at, piece_rows, 0)
        grad_total = lax.dynamic_update_slice_in_dim(grad_total, grad_old + grad_piece, where_at, 0)
        log_total = lax.dynamic_update_slice_in_dim(log_total, log_old + log_piece, where_at, 0)
        return (grad_total, log_total)
    grad_init = jnp.zeros((length + reach_rows, width), jnp.bfloat16)
    log_init = jnp.zeros((length + reach_rows,), jnp.float32)
    grad_total, log_total = lax.fori_loop(0, total_pieces, place, (grad_init, log_init))
    return (grad_total[:length], log_total[:length])

def reorder(source, source_block_plan):
    flat = source.reshape(GROUPS * BLOCKS, BLOCK, source.shape[-1])
    moved = jnp.take(flat, source_block_plan.reshape(-1).astype(jnp.int32), axis=0)
    return moved.reshape(GROUPS * BLOCKS * BLOCK, source.shape[-1])

def reference(features, frozen_query_weight, source_keys, source_values, output_gradient, adapter_down_weight, adapter_up_weight, source_block_plan, segments):
    width = HEAD_TOTAL * HEAD_SIZE
    feature_dest = reorder(features, source_block_plan)
    base_query_dest = reorder(frozen_query_weight, source_block_plan)
    keys_dest = reorder(source_keys, source_block_plan)
    values_dest = reorder(source_values, source_block_plan)
    grads_dest = output_gradient.reshape(GROUPS * LENGTH, width)
    adapter_params = jnp.dot(feature_dest, adapter_down_weight, preferred_element_type=jnp.float32).astype(jnp.bfloat16)
    query_rows = (base_query_dest.astype(jnp.float32) + jnp.dot(adapter_params, adapter_up_weight, preferred_element_type=jnp.float32)).astype(jnp.bfloat16)

    def group_pass(group_data):
        query_group, key_group, value_group, grad_group, seg_group = group_data

        def head_pass(head_index):

            def columns(array):
                return lax.dynamic_slice_in_dim(array, head_index * HEAD_SIZE, HEAD_SIZE, 1)
            return attend_head(columns(query_group), columns(key_group), columns(value_group), columns(grad_group), seg_group, CLIPS, SEG_MOST)
        return lax.map(head_pass, jnp.arange(HEAD_TOTAL, dtype=jnp.int32))
    query_gradient, log_norm = lax.map(group_pass, (query_rows.reshape(GROUPS, LENGTH, width), keys_dest.reshape(GROUPS, LENGTH, width), values_dest.reshape(GROUPS, LENGTH, width), grads_dest.reshape(GROUPS, LENGTH, width), segments))
    query_gradient = jnp.transpose(query_gradient, (0, 2, 1, 3)).reshape(GROUPS * LENGTH, width)
    adapter_gradient = lax.dot_general(query_gradient, adapter_up_weight, (((1,), (1,)), ((), ())), preferred_element_type=jnp.float32).astype(jnp.bfloat16)
    grad_norm = 4.0 / math.sqrt(GROUPS * LENGTH)
    up_grad = grad_norm * lax.dot_general(adapter_params, query_gradient, (((0,), (0,)), ((), ())), preferred_element_type=jnp.float32)
    down_grad = grad_norm * lax.dot_general(feature_dest, adapter_gradient, (((0,), (0,)), ((), ())), preferred_element_type=jnp.float32)
    return (down_grad, up_grad, log_norm)
```

```python
import functools
import math

import jax
import jax.numpy as jnp
from jax import lax
from jax.experimental import pallas as pl
from jax.experimental.pallas import tpu as pltpu
from jax.sharding import PartitionSpec as P

CAP = 2
HEAD = 128
RANK = 64
TOKENS = 4
LIVE = 20
ROWS = LIVE * TOKENS
FOLD = 48
MESH = pl.DeviceIdType.MESH
BF16 = jnp.bfloat16
F32 = jnp.float32
VMEM_LIMIT = 56 * 1024 * 1024


def block_tables(plan, group, groups):
    blocks = plan.shape[1]
    live_plan = plan[:, :LIVE]
    source = live_plan // blocks
    local = live_plan % blocks
    shift = jnp.arange(1, groups, dtype=jnp.int32)
    slot = jnp.arange(CAP, dtype=jnp.int32)
    place = jnp.arange(LIVE, dtype=jnp.int32)
    before = place[None, :] < place[:, None]

    dest = (group + shift) % groups
    dest_source = jnp.take(source, dest, axis=0)
    dest_local = jnp.take(local, dest, axis=0)
    match = dest_source == group
    rank = jnp.sum((before[None] & match[:, None, :]).astype(jnp.int32), axis=2)
    chosen = match[:, :, None] & (rank[:, :, None] == slot)
    send = jnp.sum(jnp.where(chosen, dest_local[:, :, None], 0), axis=1).reshape(-1)

    own_source = lax.dynamic_index_in_dim(source, group, 0, keepdims=False)
    own_local = lax.dynamic_index_in_dim(local, group, 0, keepdims=False)
    stays = own_source == group
    own_shift = (group - own_source + groups) % groups
    own_rank = jnp.sum((before & (own_source[None, :] == own_source[:, None])).astype(jnp.int32), axis=1)
    take = jnp.where(stays, 0, (own_shift - 1) * CAP + own_rank)
    hit = (own_shift[None, None, :] == shift[:, None, None]) & (own_rank[None, None, :] == slot[None, :, None])
    back = (LIVE + jnp.sum(jnp.where(hit, place - LIVE, 0), axis=2)).reshape(-1)
    home = jnp.where(stays, own_local, 0)
    return jnp.concatenate([send, take, back, home, stays.astype(jnp.int32)])


def exchange_kernel(
    groups, heads, tab, keys_in, values_in, base_in, grad_in, feat_in, down_ref, up_ref,
    keys_out, values_out, query_out, grad_out, adapter_out, feat_out,
    keys_pool, values_pool, query_pool, adapter_pool,
    keys_here, values_here, query_here, adapter_here, grad_buf, feat_buf,
    keys_send, values_send, query_send, adapter_send,
    keys_stage, values_stage, query_stage, grad_stage, adapter_stage, rows32, feat32, up32, adapter32,
    load_sem, own_sem, z_send, z_recv, s_send, s_recv,
):
    me_dp = lax.axis_index("dp")
    me_seq = lax.axis_index("seq")
    slots = (groups - 1) * CAP
    blocks = keys_in.shape[0]
    take_at = slots
    home_at = slots + LIVE + slots
    stay_at = home_at + LIVE

    loads = [
        pltpu.make_async_copy(keys_in, keys_here, load_sem.at[0]),
        pltpu.make_async_copy(values_in, values_here, load_sem.at[1]),
        pltpu.make_async_copy(grad_in, grad_buf, load_sem.at[2]),
        pltpu.make_async_copy(feat_in, feat_buf, load_sem.at[3]),
        pltpu.make_async_copy(base_in, query_here, load_sem.at[4]),
    ]
    for copy in loads:
        copy.start()

    barrier = pltpu.get_barrier_semaphore()

    def greet_dp(k, carry):
        pl.semaphore_signal(
            barrier, inc=1, device_id=(lax.rem(me_dp + k, groups), me_seq), device_id_type=MESH
        )
        return carry

    def greet_seq(k, carry):
        pl.semaphore_signal(
            barrier, inc=1, device_id=(me_dp, lax.rem(me_seq + k, heads)), device_id_type=MESH
        )
        return carry

    lax.fori_loop(1, groups, greet_dp, 0)
    lax.fori_loop(1, heads, greet_seq, 0)

    def pack(here, send):
        for i in range(slots):
            send[i] = here[tab[i]]

    def send_dp(send, pool, index):
        def one(k, carry):
            pltpu.make_async_remote_copy(
                src_ref=send.at[pl.ds((k - 1) * CAP, CAP)],
                dst_ref=pool.at[pl.ds((k - 1) * CAP, CAP)],
                send_sem=z_send.at[index],
                recv_sem=z_recv.at[index],
                device_id=(lax.rem(me_dp + k, groups), me_seq),
                device_id_type=MESH,
            ).start()
            return carry

        lax.fori_loop(1, groups, one, 0)

    def dp_total(send, pool, index):
        return pltpu.make_async_remote_copy(
            src_ref=send,
            dst_ref=pool,
            send_sem=z_send.at[index],
            recv_sem=z_recv.at[index],
            device_id=(lax.rem(me_dp + 1, groups), me_seq),
            device_id_type=MESH,
        )

    def send_seq(stage, out, index, same):
        def one(k, carry):
            peer = lax.rem(me_seq + k, heads)
            pltpu.make_async_remote_copy(
                src_ref=stage.at[0] if same else stage.at[peer],
                dst_ref=out.at[k],
                send_sem=s_send.at[index],
                recv_sem=s_recv.at[index],
                device_id=(me_dp, peer),
                device_id_type=MESH,
            ).start()
            return carry

        lax.fori_loop(1, heads, one, 0)
        pltpu.make_async_copy(
            stage.at[0] if same else stage.at[me_seq], out.at[0], own_sem.at[index]
        ).start()

    def seq_total(out, index):
        return pltpu.make_async_remote_copy(
            src_ref=out.at[pl.ds(1, heads - 1)],
            dst_ref=out.at[pl.ds(1, heads - 1)],
            send_sem=s_send.at[index],
            recv_sem=s_recv.at[index],
            device_id=(me_dp, lax.rem(me_seq + 1, heads)),
            device_id_type=MESH,
        )

    def to_heads(stage):
        for h in range(heads):
            stage[h] = rows32[:, h * HEAD:(h + 1) * HEAD].astype(BF16)

    def dest_block(pool, here, j):
        moved = pool[tab[take_at + j]].astype(F32)
        kept = here[tab[home_at + j]].astype(F32)
        return jnp.where(tab[stay_at + j] == 1, kept, moved)

    def unpack(pool, here, stage):
        for j in range(LIVE):
            rows32[j * TOKENS:(j + 1) * TOKENS, :] = dest_block(pool, here, j)
        to_heads(stage)

    loads[0].wait()
    pack(keys_here, keys_send)
    pl.semaphore_wait(barrier, groups + heads - 2)
    send_dp(keys_send, keys_pool, 0)
    loads[1].wait()
    pack(values_here, values_send)
    send_dp(values_send, values_pool, 1)

    loads[2].wait()
    for j in range(LIVE):
        rows32[j * TOKENS:(j + 1) * TOKENS, :] = grad_buf[j].astype(F32)
    to_heads(grad_stage)
    send_seq(grad_stage, grad_out, 3, False)

    loads[3].wait()
    loads[4].wait()
    for b in range(blocks):
        feat32[b * TOKENS:(b + 1) * TOKENS, :] = feat_buf[b].astype(F32)
    nt = (((1,), (1,)), ((), ()))
    features = feat32[: blocks * TOKENS, :].astype(BF16)
    adapter = lax.dot_general(features, down_ref[...], nt, preferred_element_type=F32).astype(BF16)
    doubled = jnp.concatenate([adapter, adapter], axis=1).astype(F32)
    adapter32[: blocks * TOKENS, :] = doubled
    up32[...] = jnp.dot(adapter, up_ref[...], preferred_element_type=F32)
    for b in range(blocks):
        query_here[b] = (
            query_here[b].astype(F32) + up32[b * TOKENS:(b + 1) * TOKENS, :]
        ).astype(BF16)
        adapter_here[b] = adapter32[b * TOKENS:(b + 1) * TOKENS, :].astype(BF16)
    pack(query_here, query_send)
    send_dp(query_send, query_pool, 2)
    pack(adapter_here, adapter_send)
    send_dp(adapter_send, adapter_pool, 3)

    for i in range(slots):
        feat32[i * TOKENS:(i + 1) * TOKENS, :] = feat_buf[tab[i]].astype(F32)
    for j in range(LIVE):
        feat32[(slots + j) * TOKENS:(slots + j + 1) * TOKENS, :] = feat_buf[tab[home_at + j]].astype(F32)
    feat_out[...] = feat32[: (slots + LIVE) * TOKENS, :].astype(BF16)

    dp_total(keys_send, keys_pool, 0).wait_recv()
    unpack(keys_pool, keys_here, keys_stage)
    send_seq(keys_stage, keys_out, 0, False)
    dp_total(values_send, values_pool, 1).wait_recv()
    unpack(values_pool, values_here, values_stage)
    send_seq(values_stage, values_out, 1, False)
    dp_total(query_send, query_pool, 2).wait_recv()
    unpack(query_pool, query_here, query_stage)
    send_seq(query_stage, query_out, 2, False)
    dp_total(adapter_send, adapter_pool, 3).wait_recv()
    adapter32[...] = jnp.zeros_like(adapter32)
    for j in range(LIVE):
        adapter32[j * TOKENS:(j + 1) * TOKENS, :] = dest_block(adapter_pool, adapter_here, j)
    lane = lax.broadcasted_iota(jnp.int32, (FOLD, HEAD), 1)
    adapter_stage[0] = jnp.where(
        lane < RANK, adapter32[0:FOLD, :], adapter32[FOLD:2 * FOLD, :]
    ).astype(BF16)
    send_seq(adapter_stage, adapter_out, 4, True)

    dp_total(keys_send, keys_pool, 0).wait_send()
    dp_total(values_send, values_pool, 1).wait_send()
    dp_total(query_send, query_pool, 2).wait_send()
    dp_total(adapter_send, adapter_pool, 3).wait_send()
    outs = (keys_out, values_out, query_out, grad_out, adapter_out)
    stages = (keys_stage, values_stage, query_stage, grad_stage, adapter_stage)
    for index in (3, 0, 1, 2, 4):
        own = stages[index].at[0]
        pltpu.make_async_copy(own, outs[index].at[0], own_sem.at[index]).wait()
        seq_total(outs[index], index).wait_recv()
        seq_total(outs[index], index).wait_send()


def exchange(tables, keys, values, base, grads, features, down_t, up, groups, heads):
    blocks = keys.shape[0]
    slots = (groups - 1) * CAP
    width = heads * HEAD
    inputs = features.shape[2]
    vmem = pl.BlockSpec(memory_space=pltpu.VMEM)
    hbm = pl.BlockSpec(memory_space=pl.ANY)
    chunk = jax.ShapeDtypeStruct((heads, ROWS, HEAD), BF16)
    feat_rows = (slots + LIVE) * TOKENS
    adapter_rows = max(blocks * TOKENS, 2 * FOLD)
    return pl.pallas_call(
        functools.partial(exchange_kernel, groups, heads),
        out_shape=(
            chunk, chunk, chunk, chunk,
            jax.ShapeDtypeStruct((heads, FOLD, HEAD), BF16),
            jax.ShapeDtypeStruct((feat_rows, inputs), BF16),
        ),
        in_specs=[pl.BlockSpec(memory_space=pltpu.SMEM)] + [hbm] * 5 + [vmem] * 2,
        out_specs=[hbm] * 5 + [vmem],
        scratch_shapes=[
            pltpu.VMEM((slots, TOKENS, width), BF16),
            pltpu.VMEM((slots, TOKENS, width), BF16),
            pltpu.VMEM((slots, TOKENS, width), BF16),
            pltpu.VMEM((slots, TOKENS, HEAD), BF16),
            pltpu.VMEM((blocks, TOKENS, width), BF16),
            pltpu.VMEM((blocks, TOKENS, width), BF16),
            pltpu.VMEM((blocks, TOKENS, width), BF16),
            pltpu.VMEM((blocks, TOKENS, HEAD), BF16),
            pltpu.VMEM((blocks, TOKENS, width), BF16),
            pltpu.VMEM((blocks, TOKENS, inputs), BF16),
            pltpu.VMEM((slots, TOKENS, width), BF16),
            pltpu.VMEM((slots, TOKENS, width), BF16),
            pltpu.VMEM((slots, TOKENS, width), BF16),
            pltpu.VMEM((slots, TOKENS, HEAD), BF16),
            pltpu.VMEM((heads, ROWS, HEAD), BF16),
            pltpu.VMEM((heads, ROWS, HEAD), BF16),
            pltpu.VMEM((heads, ROWS, HEAD), BF16),
            pltpu.VMEM((heads, ROWS, HEAD), BF16),
            pltpu.VMEM((1, FOLD, HEAD), BF16),
            pltpu.VMEM((ROWS, width), F32),
            pltpu.VMEM((max(feat_rows, blocks * TOKENS), inputs), F32),
            pltpu.VMEM((blocks * TOKENS, width), F32),
            pltpu.VMEM((adapter_rows, HEAD), F32),
            pltpu.SemaphoreType.DMA((5,)),
            pltpu.SemaphoreType.DMA((5,)),
            pltpu.SemaphoreType.DMA((4,)),
            pltpu.SemaphoreType.DMA((4,)),
            pltpu.SemaphoreType.DMA((5,)),
            pltpu.SemaphoreType.DMA((5,)),
        ],
        compiler_params=pltpu.CompilerParams(
            collective_id=1, has_side_effects=True, vmem_limit_bytes=VMEM_LIMIT
        ),
        name="exchange",
    )(tables, keys, values, base, grads, features, down_t, up)


def attention_kernel(
    heads, tile, info, query_ref, key_ref, value_ref, grad_ref, adapter_ref, up_ref,
    partial_ref, up_grad_ref, log_ref,
    key_max, key_sum, value_sum, value_neg, scores, probs, dquery, logs,
):
    total = heads * ROWS
    me_seq = info[0]
    live_count = info[1]
    scaling = 1.0 / math.sqrt(HEAD)
    to_exp2 = scaling * math.log2(math.e)
    nt = (((1,), (1,)), ((), ()))
    tn = (((0,), (0,)), ((), ()))

    def position(first, rows):
        token = first + lax.broadcasted_iota(jnp.int32, (rows, HEAD), 0)
        part = (token * 52429) >> 22
        rest = token - part * ROWS
        owner = (me_seq - part) & (heads - 1)
        return (rest >> 2) * (TOKENS * heads) + owner * TOKENS + (rest & 3)

    first_row = pl.multiple_of(me_seq * ROWS, 16)
    filler = key_ref[pl.ds(first_row, 16), :][0:1, :]
    lane = lax.broadcasted_iota(jnp.int32, (ROWS, HEAD), 1)
    for k in range(heads):
        at = slice(k * ROWS, (k + 1) * ROWS)
        live = position(k * ROWS, ROWS) < live_count
        rows = key_ref[at, :]
        zero = jnp.zeros((), BF16)
        value = jnp.where(live, value_ref[at, :], zero)
        key_max[at, :] = jnp.where(live, rows, filler)
        key_sum[at, :] = jnp.where(live, rows, zero)
        value_sum[at, 0:HEAD] = value
        value_sum[at, HEAD:] = jnp.where(live, 1.0, 0.0).astype(BF16)
        value_neg[at, 0:HEAD] = value
        value_neg[at, HEAD:] = jnp.where(lane < 3, -1.0, 0.0).astype(BF16)

    lanes = lax.broadcasted_iota(jnp.int32, (tile, HEAD), 1)

    def one_tile(index, carry):
        first = pl.multiple_of(index * tile, tile)
        query = query_ref[pl.ds(first, tile), :]
        grad = grad_ref[pl.ds(first, tile), :]
        scores[...] = lax.dot_general(query, key_max[...], nt, preferred_element_type=F32)
        maximum = jnp.max(scores[...], axis=1, keepdims=True)
        probs[...] = jnp.exp2((scores[...] - maximum) * to_exp2).astype(BF16)
        summed = jnp.dot(probs[...], value_sum[...], preferred_element_type=F32)
        norm = summed[:, HEAD:]
        inverse = 1.0 / norm
        delta = jnp.sum(grad.astype(F32) * summed[:, :HEAD], axis=1, keepdims=True) * inverse
        high = delta.astype(BF16)
        middle = (delta - high.astype(F32)).astype(BF16)
        low = (delta - high.astype(F32) - middle.astype(F32)).astype(BF16)
        zero = jnp.zeros((), BF16)
        parts = jnp.where(lanes == 0, high, jnp.where(lanes == 1, middle, jnp.where(lanes == 2, low, zero)))
        wide = jnp.concatenate([grad, parts], axis=1)
        dprob = lax.dot_general(wide, value_neg[...], nt, preferred_element_type=F32)
        dscore = (probs[...].astype(F32) * dprob).astype(BF16)
        result = jnp.dot(dscore, key_sum[...], preferred_element_type=F32) * (inverse * scaling)
        live = position(first, tile) < live_count
        dquery[pl.ds(first, tile), :] = jnp.where(live, result, 0.0).astype(BF16)
        logs[pl.ds(first, tile), :] = jnp.where(live, maximum * scaling + jnp.log(norm), 0.0)
        return carry

    lax.fori_loop(0, total // tile, one_tile, 0)

    blank = jnp.zeros((ROWS, HEAD), F32)
    gathered = blank
    row = lax.broadcasted_iota(jnp.int32, (ROWS, HEAD), 0)
    for k in range(heads):
        owner = (me_seq - k) & (heads - 1)
        column = owner * TOKENS + (row & 3)
        gathered = gathered + jnp.where(lane == column, logs[k * ROWS:(k + 1) * ROWS, :], blank)
    pick = lax.broadcasted_iota(jnp.int32, (24, ROWS), 1) >> 2
    pick = (pick == lax.broadcasted_iota(jnp.int32, (24, ROWS), 0)).astype(F32)
    log_ref[...] = jnp.dot(pick, gathered, preferred_element_type=F32, precision=lax.Precision.HIGHEST)

    up = up_ref[...]
    nothing = jnp.zeros((RANK, HEAD), BF16)
    to_low = jnp.concatenate([up, nothing], axis=0)
    to_high = jnp.concatenate([nothing, up], axis=0)
    up_total = jnp.zeros((RANK, HEAD), F32)
    for k in range(heads):
        first_part = dquery[k * ROWS:k * ROWS + FOLD, :]
        second_part = jnp.concatenate(
            [dquery[k * ROWS + FOLD:(k + 1) * ROWS, :], jnp.zeros((2 * FOLD - ROWS, HEAD), BF16)], axis=0
        )
        partial_ref[k] = (
            lax.dot_general(first_part, to_low, nt, preferred_element_type=F32)
            + lax.dot_general(second_part, to_high, nt, preferred_element_type=F32)
        ).astype(BF16)
        folded = adapter_ref[k]
        up_total = up_total + lax.dot_general(folded, first_part, tn, preferred_element_type=F32)[:RANK]
        up_total = up_total + lax.dot_general(folded, second_part, tn, preferred_element_type=F32)[RANK:]
    up_grad_ref[...] = up_total


def attention(info, query, keys, values, grads, adapter, up, heads):
    total = heads * ROWS
    tile = 256 if total % 256 == 0 else ROWS
    vmem = pl.BlockSpec(memory_space=pltpu.VMEM)
    return pl.pallas_call(
        functools.partial(attention_kernel, heads, tile),
        out_shape=(
            jax.ShapeDtypeStruct((heads, FOLD, HEAD), BF16),
            jax.ShapeDtypeStruct((RANK, HEAD), F32),
            jax.ShapeDtypeStruct((24, HEAD), F32),
        ),
        in_specs=[pl.BlockSpec(memory_space=pltpu.SMEM)] + [vmem] * 6,
        out_specs=[vmem] * 3,
        scratch_shapes=[
            pltpu.VMEM((total, HEAD), BF16),
            pltpu.VMEM((total, HEAD), BF16),
            pltpu.VMEM((total, 2 * HEAD), BF16),
            pltpu.VMEM((total, 2 * HEAD), BF16),
            pltpu.VMEM((tile, total), F32),
            pltpu.VMEM((tile, total), BF16),
            pltpu.VMEM((total, HEAD), BF16),
            pltpu.VMEM((total, HEAD), F32),
        ],
        compiler_params=pltpu.CompilerParams(vmem_limit_bytes=VMEM_LIMIT),
        name="attention",
    )(info, query, keys, values, grads, adapter, up)


def reduce_kernel(
    groups, heads, scale, tab, partial_ref, up_ref, feat_ref,
    down_out, up_out,
    partial_recv, blocks32, pieces, grads_send, grads_recv, down_send, down_recv,
    share_send, share_recv, up_recv,
    s_send, s_recv, z_send, z_recv,
):
    me_dp = lax.axis_index("dp")
    me_seq = lax.axis_index("seq")
    slots = (groups - 1) * CAP
    back_at = slots + LIVE
    stay_at = back_at + slots + LIVE
    tn = (((0,), (0,)), ((), ()))

    barrier = pltpu.get_barrier_semaphore()

    def greet_dp(k, carry):
        pl.semaphore_signal(
            barrier, inc=1, device_id=(lax.rem(me_dp + k, groups), me_seq), device_id_type=MESH
        )
        return carry

    def greet_seq(k, carry):
        pl.semaphore_signal(
            barrier, inc=1, device_id=(me_dp, lax.rem(me_seq + k, heads)), device_id_type=MESH
        )
        return carry

    lax.fori_loop(1, groups, greet_dp, 0)
    lax.fori_loop(1, heads, greet_seq, 0)
    pl.semaphore_wait(barrier, groups + heads - 2)

    def seq_copy(k, src, dst, index):
        return pltpu.make_async_remote_copy(
            src_ref=src, dst_ref=dst, send_sem=s_send.at[index], recv_sem=s_recv.at[index],
            device_id=(me_dp, k), device_id_type=MESH,
        )

    def dp_copy(k, src, dst, index):
        return pltpu.make_async_remote_copy(
            src_ref=src, dst_ref=dst, send_sem=z_send.at[index], recv_sem=z_recv.at[index],
            device_id=(k, me_seq), device_id_type=MESH,
        )

    def send_partial(k, carry):
        seq_copy(lax.rem(me_seq + heads - k, heads), partial_ref.at[k], partial_recv.at[k - 1], 0).start()
        return carry

    lax.fori_loop(1, heads, send_partial, 0)

    def send_up(k, carry):
        dp_copy(lax.rem(me_dp + k, groups), up_ref, up_recv.at[k - 1], 0).start()
        return carry

    lax.fori_loop(1, groups, send_up, 0)

    partial_total = seq_copy(lax.rem(me_seq + 1, heads), partial_ref.at[pl.ds(1, heads - 1)], partial_recv, 0)
    partial_total.wait_recv()
    folded = partial_ref[0].astype(F32)
    for k in range(heads - 1):
        folded = folded + partial_recv[k].astype(F32)
    turned = pltpu.roll(folded, RANK, 1)
    for j in range(LIVE):
        row = j * TOKENS
        from_ref = folded if row < FOLD else turned
        row = row if row < FOLD else row - FOLD
        blocks32[j] = from_ref[row:row + TOKENS, :]
    blocks32[LIVE] = jnp.zeros((TOKENS, HEAD), F32)

    for i in range(slots):
        k, slot = i // CAP, i % CAP
        grads_send[k, slot * TOKENS:(slot + 1) * TOKENS, :] = blocks32[tab[back_at + i]]

    def send_grads(k, carry):
        dp_copy(lax.rem(me_dp + groups - k, groups), grads_send.at[k - 1], grads_recv.at[k - 1], 1).start()
        return carry

    lax.fori_loop(1, groups, send_grads, 0)
    for j in range(LIVE):
        stays = (tab[stay_at + j]).astype(F32)
        pieces[slots * TOKENS + j * TOKENS:slots * TOKENS + (j + 1) * TOKENS, :] = blocks32[j] * stays
    grads_total = dp_copy(lax.rem(me_dp + 1, groups), grads_send, grads_recv, 1)
    grads_total.wait_recv()
    for k in range(groups - 1):
        pieces[k * 2 * TOKENS:(k + 1) * 2 * TOKENS, :] = grads_recv[k]

    adapter_grad = pieces[...].astype(BF16)[:, :RANK]
    doubled = jnp.concatenate([adapter_grad, adapter_grad], axis=1)
    lane = lax.broadcasted_iota(jnp.int32, (FOLD, HEAD), 1)
    transposed = lax.dot_general(doubled, feat_ref[...], tn, preferred_element_type=F32)
    down = transposed.T
    for h in range(heads):
        first = down[h * ROWS:h * ROWS + FOLD, :]
        second = jnp.concatenate(
            [down[h * ROWS + FOLD:(h + 1) * ROWS, :], jnp.zeros((2 * FOLD - ROWS, HEAD), F32)], axis=0
        )
        down_send[h] = jnp.where(lane < RANK, first, second).astype(BF16)

    def send_down(k, carry):
        peer = lax.rem(me_seq + k, heads)
        seq_copy(peer, down_send.at[peer], down_recv.at[k - 1], 1).start()
        return carry

    lax.fori_loop(1, heads, send_down, 0)
    down_total = seq_copy(lax.rem(me_seq + 1, heads), down_send.at[pl.ds(0, heads - 1)], down_recv, 1)
    down_total.wait_recv()
    share = down_send[me_seq].astype(F32)
    for k in range(heads - 1):
        share = share + down_recv[k].astype(F32)
    share_send[...] = share

    def send_share(k, carry):
        dp_copy(lax.rem(me_dp + k, groups), share_send, share_recv.at[k - 1], 2).start()
        return carry

    lax.fori_loop(1, groups, send_share, 0)
    up_total = dp_copy(lax.rem(me_dp + 1, groups), up_recv, up_recv, 0)
    up_total.wait_recv()
    up_sum = up_ref[...]
    for k in range(groups - 1):
        up_sum = up_sum + up_recv[k]
    up_out[...] = up_sum * scale
    share_total = dp_copy(lax.rem(me_dp + 1, groups), share_recv, share_recv, 2)
    share_total.wait_recv()
    for k in range(groups - 1):
        share = share + share_recv[k]
    share = share * scale
    turned = pltpu.roll(share, RANK, 1)
    whole = jnp.concatenate(
        [share, turned[:ROWS - FOLD], jnp.zeros((HEAD - ROWS, HEAD), F32)], axis=0
    )
    down_out[...] = whole.T[:RANK, :ROWS]

    partial_total.wait_send()
    up_total.wait_send()
    grads_total.wait_send()
    down_total.wait_send()
    share_total.wait_send()


def reduce_gradients(tables, partial, up_part, feat_rows, scale, groups, heads):
    slots = (groups - 1) * CAP
    vmem = pl.BlockSpec(memory_space=pltpu.VMEM)
    return pl.pallas_call(
        functools.partial(reduce_kernel, groups, heads, scale),
        out_shape=(
            jax.ShapeDtypeStruct((RANK, ROWS), F32),
            jax.ShapeDtypeStruct((RANK, HEAD), F32),
        ),
        in_specs=[pl.BlockSpec(memory_space=pltpu.SMEM)] + [vmem] * 3,
        out_specs=[vmem] * 2,
        scratch_shapes=[
            pltpu.VMEM((heads - 1, FOLD, HEAD), BF16),
            pltpu.VMEM((LIVE + 1, TOKENS, HEAD), F32),
            pltpu.VMEM(((slots + LIVE) * TOKENS, HEAD), F32),
            pltpu.VMEM((groups - 1, CAP * TOKENS, HEAD), F32),
            pltpu.VMEM((groups - 1, CAP * TOKENS, HEAD), F32),
            pltpu.VMEM((heads, FOLD, HEAD), BF16),
            pltpu.VMEM((heads - 1, FOLD, HEAD), BF16),
            pltpu.VMEM((FOLD, HEAD), F32),
            pltpu.VMEM((groups - 1, FOLD, HEAD), F32),
            pltpu.VMEM((groups - 1, RANK, HEAD), F32),
            pltpu.SemaphoreType.DMA((2,)),
            pltpu.SemaphoreType.DMA((2,)),
            pltpu.SemaphoreType.DMA((3,)),
            pltpu.SemaphoreType.DMA((3,)),
        ],
        compiler_params=pltpu.CompilerParams(
            collective_id=2, has_side_effects=True, vmem_limit_bytes=VMEM_LIMIT
        ),
        name="reduce_gradients",
    )(tables, partial, up_part, feat_rows)


def per_device(
    features, frozen_query_weight, source_keys, source_values, output_gradient,
    adapter_down_weight, adapter_up_weight, source_block_plan, segments,
):
    groups = lax.axis_size("dp")
    heads = lax.axis_size("seq")
    group = lax.axis_index("dp")
    head = lax.axis_index("seq")
    tables = block_tables(source_block_plan, group, groups)
    live_count = jnp.sum((segments[0] < 1).astype(jnp.int32))
    info = jnp.stack([head.astype(jnp.int32), live_count])
    keys, values, query, grads, adapter, feat_rows = exchange(
        tables, source_keys[0], source_values[0], frozen_query_weight[0], output_gradient[0], features[0],
        adapter_down_weight.T, adapter_up_weight, groups, heads,
    )
    total = heads * ROWS
    up_head = lax.dynamic_slice_in_dim(adapter_up_weight, head * HEAD, HEAD, 1)
    partial, up_part, logs = attention(
        info, query.reshape(total, HEAD), keys.reshape(total, HEAD), values.reshape(total, HEAD),
        grads.reshape(total, HEAD), adapter, up_head, heads,
    )
    length = segments.shape[1]
    scale = 4.0 / math.sqrt(groups * length)
    down, up = reduce_gradients(tables, partial, up_part, feat_rows, scale, groups, heads)
    log_norm = logs[:LIVE, : TOKENS * heads].reshape(-1)
    log_norm = jnp.pad(log_norm, (0, length - log_norm.shape[0]))
    return (down.T, up, log_norm[None, None])


def solution(mesh):
    in_specs = (
        P("dp", None, "seq", None),
        P("dp", None, "seq", None),
        P("dp", None, "seq", None),
        P("dp", None, "seq", None),
        P("dp", None, "seq", None),
        P(),
        P(),
        P(),
        P("dp", None),
    )
    out_specs = (P("seq", None), P(None, "seq"), P("dp", "seq", None))
    return jax.shard_map(
        per_device, mesh=mesh, in_specs=in_specs, out_specs=out_specs, check_vma=False
    )
```

```python
import functools
import math

import jax
import jax.numpy as jnp
from jax import lax
from jax.experimental import pallas as pl
from jax.experimental.pallas import tpu as pltpu
from jax.sharding import PartitionSpec as P

CAP = 2
HEAD = 128
RANK = 64
TOKENS = 4
LIVE = 20
ROWS = LIVE * TOKENS
PARTS = 4
FOLD = 48
MESH = pl.DeviceIdType.MESH
BF16 = jnp.bfloat16
F32 = jnp.float32
VMEM_LIMIT = 56 * 1024 * 1024


def tables_kernel(groups, plan_ref, tab_ref):
    group = lax.axis_index("dp")
    blocks = plan_ref.shape[1]
    shift = blocks.bit_length() - 1
    plan = plan_ref[...]
    source, local = plan >> shift, plan & (blocks - 1)
    row = lax.broadcasted_iota(jnp.int32, (groups, blocks), 0)
    place = lax.broadcasted_iota(jnp.int32, (groups, blocks), 1)
    live = place < LIVE
    first = lax.broadcasted_iota(jnp.int32, (blocks, blocks), 0)
    second = lax.broadcasted_iota(jnp.int32, (blocks, blocks), 1)
    match = live & (source == group)
    rank = jnp.dot(match.astype(F32), (first < second).astype(F32), preferred_element_type=F32)

    def column(chosen, value):
        return jnp.sum(jnp.where(chosen, value, 0), axis=1, keepdims=True)

    send = [column(match & (rank == r), local) for r in range(CAP)]
    own = jnp.sum(jnp.where(row == group, plan, 0), axis=0, keepdims=True)
    own_source, own_local = own >> shift, own & (blocks - 1)
    down_column = jnp.sum(jnp.where(first == second, own_source, 0), axis=1, keepdims=True)
    same = (down_column == own_source) & (first < second)
    own_rank = jnp.sum(same.astype(jnp.int32), axis=0, keepdims=True)
    back = [
        LIVE + column(live & (own_source == row) & (own_rank == r), place - LIVE) for r in range(CAP)
    ]
    stays = own_source == group
    distance = (group - own_source + groups) & (groups - 1)
    take = jnp.where(stays, 0, (distance - 1) * CAP + own_rank)
    tab_ref[...] = jnp.zeros_like(tab_ref)
    for at, part in enumerate(send + back):
        tab_ref[0:groups, at:at + 1] = part
    tab_ref[groups:groups + 1, 0:blocks] = take
    tab_ref[groups + 1:groups + 2, 0:blocks] = jnp.where(stays, own_local, 0)
    tab_ref[groups + 2:groups + 3, 0:blocks] = stays.astype(jnp.int32)


def block_tables(plan, groups):
    vmem = pl.BlockSpec(memory_space=pltpu.VMEM)
    return pl.pallas_call(
        functools.partial(tables_kernel, groups),
        out_shape=jax.ShapeDtypeStruct((24, HEAD), jnp.int32),
        in_specs=[vmem],
        out_specs=vmem,
        name="tables",
    )(plan)


def greet_all(groups, heads, me_dp, me_seq):
    barrier = pltpu.get_barrier_semaphore()

    def greet_dp(k, carry):
        pl.semaphore_signal(
            barrier, inc=1, device_id=(lax.rem(me_dp + k, groups), me_seq), device_id_type=MESH
        )
        return carry

    def greet_seq(k, carry):
        pl.semaphore_signal(
            barrier, inc=1, device_id=(me_dp, lax.rem(me_seq + k, heads)), device_id_type=MESH
        )
        return carry

    lax.fori_loop(1, groups, greet_dp, 0)
    lax.fori_loop(1, heads, greet_seq, 0)
    return barrier


def exchange_kernel(
    groups, heads, parts, tab, keys_in, values_in, base_in, grad_in, feat_in, down_ref, up_ref,
    keys_out, values_out, query_out, grad_out, adapter_out, feat_moving, feat_staying,
    *scratch,
):
    keys_pool, values_pool, query_pool = (scratch[n * parts:(n + 1) * parts] for n in range(3))
    (
        adapter_pool,
        keys_here, values_here, query_here, adapter_here, grad_buf, feat_buf,
        keys_send, values_send, query_send, adapter_send,
        keys_stage, values_stage, query_stage, grad_stage, adapter_stage, rows32, feat32, up32, adapter32,
        load_sem, own_sem, z_send, z_recv, s_send, s_recv,
    ) = scratch[3 * parts:]
    me_dp = lax.axis_index("dp")
    me_seq = lax.axis_index("seq")
    slots = (groups - 1) * CAP
    blocks = keys_in.shape[0]
    per_part = heads // parts

    def head_of(part, c):
        return c * parts + ((part - c) & (parts - 1))

    def slot_source(i):
        return tab[lax.rem(me_dp + 1 + i // CAP, groups), i % CAP]

    loads = [
        pltpu.make_async_copy(keys_in, keys_here, load_sem.at[0]),
        pltpu.make_async_copy(base_in, query_here, load_sem.at[1]),
        pltpu.make_async_copy(feat_in, feat_buf, load_sem.at[2]),
        pltpu.make_async_copy(grad_in, grad_buf, load_sem.at[3]),
        pltpu.make_async_copy(values_in, values_here, load_sem.at[4]),
    ]
    for copy in loads:
        copy.start()
    barrier = greet_all(groups, heads, me_dp, me_seq)

    def pack(here, send):
        for i in range(slots):
            block = here[slot_source(i)]
            for part in range(parts):
                for c in range(per_part):
                    h = head_of(part, c)
                    send[part, i, :, c * HEAD:(c + 1) * HEAD] = block[:, h * HEAD:(h + 1) * HEAD]

    def send_dp(send, pool, index):
        def one(k, carry):
            pltpu.make_async_remote_copy(
                src_ref=send.at[pl.ds((k - 1) * CAP, CAP)],
                dst_ref=pool.at[pl.ds((k - 1) * CAP, CAP)],
                send_sem=z_send.at[index],
                recv_sem=z_recv.at[index],
                device_id=(lax.rem(me_dp + k, groups), me_seq),
                device_id_type=MESH,
            ).start()
            return carry

        lax.fori_loop(1, groups, one, 0)

    def dp_total(send, pool, index):
        return pltpu.make_async_remote_copy(
            src_ref=send,
            dst_ref=pool,
            send_sem=z_send.at[index],
            recv_sem=z_recv.at[index],
            device_id=(lax.rem(me_dp + 1, groups), me_seq),
            device_id_type=MESH,
        )

    def send_seq(src, out, index, peer):
        @pl.when(peer != me_seq)
        def _():
            pltpu.make_async_remote_copy(
                src_ref=src,
                dst_ref=out.at[lax.rem(peer + heads - me_seq, heads)],
                send_sem=s_send.at[index],
                recv_sem=s_recv.at[index],
                device_id=(me_dp, peer),
                device_id_type=MESH,
            ).start()

        @pl.when(peer == me_seq)
        def _():
            pltpu.make_async_copy(src, out.at[0], own_sem.at[index]).start()

    def send_part(stage, out, index, part):
        def one(step, carry):
            c = lax.rem(step + 1 + me_seq // parts, per_part)
            peer = head_of(part, c)
            send_seq(stage.at[peer], out, index, peer)
            return carry

        lax.fori_loop(0, per_part, one, 0)

    def seq_total(out, index):
        return pltpu.make_async_remote_copy(
            src_ref=out.at[pl.ds(1, heads - 1)],
            dst_ref=out.at[pl.ds(1, heads - 1)],
            send_sem=s_send.at[index],
            recv_sem=s_recv.at[index],
            device_id=(me_dp, lax.rem(me_seq + 1, heads)),
            device_id_type=MESH,
        )

    def dest_block(moved, kept, j):
        return jnp.where(tab[groups + 2, j] == 1, kept.astype(F32), moved.astype(F32))

    def pass_on(pool, here, stage, out, index, part):
        for j in range(LIVE):
            kept = here[tab[groups + 1, j]]
            kept = jnp.concatenate(
                [kept[:, h * HEAD:(h + 1) * HEAD] for h in [head_of(part, c) for c in range(per_part)]], axis=1
            )
            rows32[j * TOKENS:(j + 1) * TOKENS, : per_part * HEAD] = dest_block(
                pool[part][tab[groups, j]], kept, j
            )
        for c in range(per_part):
            stage[head_of(part, c)] = rows32[:, c * HEAD:(c + 1) * HEAD].astype(BF16)
        send_part(stage, out, index, part)

    loads[0].wait()
    pack(keys_here, keys_send)
    pl.semaphore_wait(barrier, groups + heads - 2)
    for part in range(parts):
        send_dp(keys_send.at[part], keys_pool[part], part)

    loads[3].wait()
    for j in range(LIVE):
        rows32[j * TOKENS:(j + 1) * TOKENS, :] = grad_buf[j].astype(F32)
    for h in range(heads):
        grad_stage[h] = rows32[:, h * HEAD:(h + 1) * HEAD].astype(BF16)
    for part in range(parts):
        send_part(grad_stage, grad_out, 3, part)

    loads[1].wait()
    loads[2].wait()
    for b in range(blocks):
        feat32[b * TOKENS:(b + 1) * TOKENS, :] = feat_buf[b].astype(F32)
    nt = (((1,), (1,)), ((), ()))
    features = feat32[: blocks * TOKENS, :].astype(BF16)
    adapter = lax.dot_general(features, down_ref[...], nt, preferred_element_type=F32).astype(BF16)
    adapter32[: blocks * TOKENS, :] = jnp.concatenate([adapter, adapter], axis=1).astype(F32)
    up32[...] = jnp.dot(adapter, up_ref[...], preferred_element_type=F32)
    for b in range(blocks):
        query_here[b] = (query_here[b].astype(F32) + up32[b * TOKENS:(b + 1) * TOKENS, :]).astype(BF16)
        adapter_here[b] = adapter32[b * TOKENS:(b + 1) * TOKENS, :].astype(BF16)
    pack(query_here, query_send)
    for i in range(slots):
        adapter_send[i] = adapter_here[slot_source(i)]
    send_dp(adapter_send, adapter_pool, 3 * parts)
    for part in range(parts):
        send_dp(query_send.at[part], query_pool[part], parts + part)
    loads[4].wait()
    pack(values_here, values_send)
    for part in range(parts):
        send_dp(values_send.at[part], values_pool[part], 2 * parts + part)

    for i in range(slots):
        feat32[i * TOKENS:(i + 1) * TOKENS, :] = feat_buf[slot_source(i)].astype(F32)
    for k in range(groups - 1):
        feat_moving[k] = feat32[k * CAP * TOKENS:(k + 1) * CAP * TOKENS, :].astype(BF16)
    for j in range(LIVE):
        feat32[j * TOKENS:(j + 1) * TOKENS, :] = feat_buf[tab[groups + 1, j]].astype(F32)
    feat_staying[...] = feat32[:ROWS, :].astype(BF16)

    for part in range(parts):
        dp_total(keys_send.at[part], keys_pool[part], part).wait_recv()
        pass_on(keys_pool, keys_here, keys_stage, keys_out, 0, part)
    dp_total(adapter_send, adapter_pool, 3 * parts).wait_recv()
    adapter32[...] = jnp.zeros_like(adapter32)
    for j in range(LIVE):
        adapter32[j * TOKENS:(j + 1) * TOKENS, :] = dest_block(
            adapter_pool[tab[groups, j]], adapter_here[tab[groups + 1, j]], j
        )
    lane = lax.broadcasted_iota(jnp.int32, (FOLD, HEAD), 1)
    adapter_stage[...] = jnp.where(
        lane < RANK, adapter32[0:FOLD, :], adapter32[FOLD:2 * FOLD, :]
    ).astype(BF16)

    def spread(k, carry):
        send_seq(adapter_stage, adapter_out, 4, lax.rem(me_seq + k, heads))
        return carry

    lax.fori_loop(0, heads, spread, 0)
    for part in range(parts):
        dp_total(query_send.at[part], query_pool[part], parts + part).wait_recv()
        pass_on(query_pool, query_here, query_stage, query_out, 2, part)
    for part in range(parts):
        dp_total(values_send.at[part], values_pool[part], 2 * parts + part).wait_recv()
        pass_on(values_pool, values_here, values_stage, values_out, 1, part)

    for part in range(parts):
        dp_total(keys_send.at[part], keys_pool[part], part).wait_send()
        dp_total(query_send.at[part], query_pool[part], parts + part).wait_send()
        dp_total(values_send.at[part], values_pool[part], 2 * parts + part).wait_send()
    dp_total(adapter_send, adapter_pool, 3 * parts).wait_send()
    outs = (keys_out, values_out, query_out, grad_out, adapter_out)
    stages = (keys_stage, values_stage, query_stage, grad_stage, None)
    for index in (3, 0, 4, 2, 1):
        out = outs[index]
        own = adapter_stage if stages[index] is None else stages[index].at[0]
        pltpu.make_async_copy(own, out.at[0], own_sem.at[index]).wait()
        seq_total(out, index).wait_recv()
        seq_total(out, index).wait_send()


def exchange(tables, keys, values, base, grads, features, down_t, up, groups, heads):
    blocks = keys.shape[0]
    slots = (groups - 1) * CAP
    width = heads * HEAD
    parts = min(PARTS, heads)
    inputs = features.shape[2]
    vmem = pl.BlockSpec(memory_space=pltpu.VMEM)
    hbm = pl.BlockSpec(memory_space=pl.ANY)
    chunk = jax.ShapeDtypeStruct((heads, ROWS, HEAD), BF16)
    feat_rows = max(slots, LIVE, blocks) * TOKENS
    adapter_rows = max(blocks * TOKENS, 2 * FOLD)
    arriving = pltpu.VMEM((slots, TOKENS, width // parts), BF16)
    moving = pltpu.VMEM((parts, slots, TOKENS, width // parts), BF16)
    here = pltpu.VMEM((blocks, TOKENS, width), BF16)
    stage = pltpu.VMEM((heads, ROWS, HEAD), BF16)
    return pl.pallas_call(
        functools.partial(exchange_kernel, groups, heads, parts),
        out_shape=(
            chunk, chunk, chunk, chunk,
            jax.ShapeDtypeStruct((heads, FOLD, HEAD), BF16),
            jax.ShapeDtypeStruct((groups - 1, CAP * TOKENS, inputs), BF16),
            jax.ShapeDtypeStruct((ROWS, inputs), BF16),
        ),
        in_specs=[pl.BlockSpec(memory_space=pltpu.SMEM)] + [hbm] * 5 + [vmem] * 2,
        out_specs=[hbm] * 5 + [vmem] * 2,
        scratch_shapes=[arriving] * (3 * parts) + [
            pltpu.VMEM((slots, TOKENS, HEAD), BF16),
            here, here, here,
            pltpu.VMEM((blocks, TOKENS, HEAD), BF16),
            here,
            pltpu.VMEM((blocks, TOKENS, inputs), BF16),
            moving, moving, moving,
            pltpu.VMEM((slots, TOKENS, HEAD), BF16),
            stage, stage, stage, stage,
            pltpu.VMEM((FOLD, HEAD), BF16),
            pltpu.VMEM((ROWS, width), F32),
            pltpu.VMEM((feat_rows, inputs), F32),
            pltpu.VMEM((blocks * TOKENS, width), F32),
            pltpu.VMEM((adapter_rows, HEAD), F32),
            pltpu.SemaphoreType.DMA((5,)),
            pltpu.SemaphoreType.DMA((5,)),
            pltpu.SemaphoreType.DMA((3 * parts + 1,)),
            pltpu.SemaphoreType.DMA((3 * parts + 1,)),
            pltpu.SemaphoreType.DMA((5,)),
            pltpu.SemaphoreType.DMA((5,)),
        ],
        compiler_params=pltpu.CompilerParams(
            collective_id=1, has_side_effects=True, vmem_limit_bytes=VMEM_LIMIT
        ),
        name="exchange",
    )(tables, keys, values, base, grads, features, down_t, up)


def attend_kernel(
    groups, heads, tile, scale, tab, segments_ref, up_ref, query_ref, key_ref, value_ref, grad_ref, adapter_ref,
    feat_moving, feat_staying,
    down_out, up_out, log_ref,
    key_max, key_sum, value_sum, value_neg, scores, probs, dquery, logs, up_head,
    feat_recv, feat32, partial_send, partial_recv, blocks32, pieces, down_send, down_recv,
    up_send, up_recv, total_send, total_recv, whole32, share_recv,
    up_sem, s_send, s_recv, z_send, z_recv,
):
    total = heads * ROWS
    me_dp = lax.axis_index("dp")
    me_seq = lax.axis_index("seq")
    slots = (groups - 1) * CAP
    up_rows = RANK // groups
    scaling = 1.0 / math.sqrt(HEAD)
    to_exp2 = scaling * math.log2(math.e)
    nt = (((1,), (1,)), ((), ()))
    tn = (((0,), (0,)), ((), ()))
    zero = jnp.zeros((), BF16)

    def seq_copy(k, src, dst, index):
        return pltpu.make_async_remote_copy(
            src_ref=src, dst_ref=dst, send_sem=s_send.at[index], recv_sem=s_recv.at[index],
            device_id=(me_dp, k), device_id_type=MESH,
        )

    def dp_copy(k, src, dst, index):
        return pltpu.make_async_remote_copy(
            src_ref=src, dst_ref=dst, send_sem=z_send.at[index], recv_sem=z_recv.at[index],
            device_id=(k, me_seq), device_id_type=MESH,
        )

    barrier = greet_all(groups, heads, me_dp, me_seq)
    up_copy = pltpu.make_async_copy(
        up_ref.at[:, pl.ds(pl.multiple_of(me_seq * HEAD, HEAD), HEAD)], up_head, up_sem
    )
    up_copy.start()
    live_count = jnp.sum((segments_ref[...] < 1).astype(jnp.int32), axis=1, keepdims=True)

    def position(first, rows):
        token = first + lax.broadcasted_iota(jnp.int32, (rows, HEAD), 0)
        part = (token * 52429) >> 22
        rest = token - part * ROWS
        owner = (me_seq - part) & (heads - 1)
        return (rest >> 2) * (TOKENS * heads) + owner * TOKENS + (rest & 3)

    first_row = pl.multiple_of(me_seq * ROWS, 16)
    filler = key_ref[pl.ds(first_row, 16), :][0:1, :]
    lane = lax.broadcasted_iota(jnp.int32, (ROWS, HEAD), 1)
    for k in range(heads):
        at = slice(k * ROWS, (k + 1) * ROWS)
        live = position(k * ROWS, ROWS) < live_count
        rows = key_ref[at, :]
        value = jnp.where(live, value_ref[at, :], zero)
        key_max[at, :] = jnp.where(live, rows, filler)
        key_sum[at, :] = jnp.where(live, rows, zero)
        value_sum[at, 0:HEAD] = value
        value_sum[at, HEAD:] = jnp.where(live, 1.0, 0.0).astype(BF16)
        value_neg[at, 0:HEAD] = value
        value_neg[at, HEAD:] = jnp.where(lane < 3, -1.0, 0.0).astype(BF16)

    up_copy.wait()
    up = up_head[...]
    nothing = jnp.zeros((RANK, HEAD), BF16)
    to_low = jnp.concatenate([up, nothing], axis=0)
    to_high = jnp.concatenate([nothing, up], axis=0)
    filling = jnp.zeros((2 * FOLD - ROWS, HEAD), BF16)

    pl.semaphore_wait(barrier, groups + heads - 2)

    def send_features(k, carry):
        dp_copy(lax.rem(me_dp + k, groups), feat_moving.at[k - 1], feat_recv.at[k - 1], 0).start()
        return carry

    lax.fori_loop(1, groups, send_features, 0)
    lanes = lax.broadcasted_iota(jnp.int32, (tile, HEAD), 1)

    def one_tile(index, carry):
        first = pl.multiple_of(index * tile, tile)
        query = query_ref[pl.ds(first, tile), :]
        grad = grad_ref[pl.ds(first, tile), :]
        scores[...] = lax.dot_general(query, key_max[...], nt, preferred_element_type=F32)
        maximum = jnp.max(scores[...], axis=1, keepdims=True)
        probs[...] = jnp.exp2((scores[...] - maximum) * to_exp2).astype(BF16)
        summed = jnp.dot(probs[...], value_sum[...], preferred_element_type=F32)
        norm = summed[:, HEAD:]
        inverse = 1.0 / norm
        delta = jnp.sum(grad.astype(F32) * summed[:, :HEAD], axis=1, keepdims=True) * inverse
        high = delta.astype(BF16)
        middle = (delta - high.astype(F32)).astype(BF16)
        low = (delta - high.astype(F32) - middle.astype(F32)).astype(BF16)
        split = jnp.where(lanes == 0, high, jnp.where(lanes == 1, middle, jnp.where(lanes == 2, low, zero)))
        wide = jnp.concatenate([grad, split], axis=1)
        dprob = lax.dot_general(wide, value_neg[...], nt, preferred_element_type=F32)
        dscore = (probs[...].astype(F32) * dprob).astype(BF16)
        result = jnp.dot(dscore, key_sum[...], preferred_element_type=F32) * (inverse * scaling)
        live = position(first, tile) < live_count
        result = jnp.where(live, result, 0.0).astype(BF16)
        dquery[pl.ds(first, tile), :] = result
        logs[pl.ds(first, tile), :] = jnp.where(live, maximum * scaling + jnp.log(norm), 0.0)
        for c in range(tile // ROWS):
            k = index * (tile // ROWS) + c
            first_part = result[c * ROWS:c * ROWS + FOLD]
            second_part = jnp.concatenate([result[c * ROWS + FOLD:(c + 1) * ROWS], filling], axis=0)
            partial_send[k] = (
                lax.dot_general(first_part, to_low, nt, preferred_element_type=F32)
                + lax.dot_general(second_part, to_high, nt, preferred_element_type=F32)
            ).astype(BF16)

            @pl.when(k > 0)
            def _():
                seq_copy(
                    lax.rem(me_seq + heads - k, heads), partial_send.at[k], partial_recv.at[k - 1], 0
                ).start()

        return carry

    lax.fori_loop(0, total // tile, one_tile, 0)

    up_total = jnp.zeros((RANK, HEAD), F32)
    for k in range(heads):
        first_part = dquery[k * ROWS:k * ROWS + FOLD, :]
        second_part = jnp.concatenate([dquery[k * ROWS + FOLD:(k + 1) * ROWS, :], filling], axis=0)
        folded = adapter_ref[k]
        up_total = up_total + lax.dot_general(folded, first_part, tn, preferred_element_type=F32)[:RANK]
        up_total = up_total + lax.dot_general(folded, second_part, tn, preferred_element_type=F32)[RANK:]
    up_send[...] = jnp.zeros_like(up_send)
    for d in range(groups):
        up_send[d, 0:up_rows, :] = up_total[d * up_rows:(d + 1) * up_rows, :]

    def send_up(k, carry):
        peer = lax.rem(me_dp + k, groups)
        dp_copy(peer, up_send.at[peer], up_recv.at[k - 1], 1).start()
        return carry

    lax.fori_loop(1, groups, send_up, 0)

    def dp_total(like, index):
        return dp_copy(lax.rem(me_dp + 1, groups), like, like, index)

    dp_total(feat_recv, 0).wait_recv()
    for k in range(groups - 1):
        feat32[k * CAP * TOKENS:(k + 1) * CAP * TOKENS, :] = feat_recv[k].astype(F32)
    moved_rows = feat32[...].astype(BF16)

    partial_total = seq_copy(lax.rem(me_seq + 1, heads), partial_send.at[pl.ds(1, heads - 1)], partial_recv, 0)
    partial_total.wait_recv()
    folded = partial_send[0].astype(F32)
    for k in range(heads - 1):
        folded = folded + partial_recv[k].astype(F32)
    turned = pltpu.roll(folded, RANK, 1)
    for j in range(LIVE):
        row = j * TOKENS
        half = folded if row < FOLD else turned
        row = row if row < FOLD else row - FOLD
        blocks32[j] = half[row:row + TOKENS, :]
    blocks32[LIVE] = jnp.zeros((TOKENS, HEAD), F32)
    for k in range(1, groups):
        origin = lax.rem(me_dp + groups - k, groups)
        for r in range(CAP):
            row = ((k - 1) * CAP + r) * TOKENS
            pieces[row:row + TOKENS, :] = blocks32[tab[origin, CAP + r]]
    for j in range(LIVE):
        stays = tab[groups + 2, j].astype(F32)
        pieces[(slots + j) * TOKENS:(slots + j + 1) * TOKENS, :] = blocks32[j] * stays
    own_lane = lax.broadcasted_iota(jnp.int32, pieces.shape, 1)
    grads = pieces[...]
    doubled = jnp.where(own_lane < RANK, grads, pltpu.roll(grads, RANK, 1)).astype(BF16)
    down = lax.dot_general(doubled[:slots * TOKENS], moved_rows, tn, preferred_element_type=F32)
    down = down + lax.dot_general(doubled[slots * TOKENS:], feat_staying[...], tn, preferred_element_type=F32)
    down = down.T
    fold_lane = lax.broadcasted_iota(jnp.int32, (FOLD, HEAD), 1)
    for h in range(heads):
        first = down[h * ROWS:h * ROWS + FOLD, :]
        second = jnp.concatenate(
            [down[h * ROWS + FOLD:(h + 1) * ROWS, :], jnp.zeros((2 * FOLD - ROWS, HEAD), F32)], axis=0
        )
        down_send[h] = jnp.where(fold_lane < RANK, first, second).astype(BF16)

    def send_down(k, carry):
        peer = lax.rem(me_seq + k, heads)
        seq_copy(peer, down_send.at[peer], down_recv.at[k - 1], 1).start()
        return carry

    lax.fori_loop(1, heads, send_down, 0)

    dp_total(up_recv, 1).wait_recv()
    up_sum = up_send[me_dp]
    for k in range(groups - 1):
        up_sum = up_sum + up_recv[k]
    total_send[...] = up_sum * scale

    def send_total(k, carry):
        dp_copy(lax.rem(me_dp + k, groups), total_send, total_recv.at[k - 1], 2).start()
        return carry

    lax.fori_loop(1, groups, send_total, 0)
    gathered = jnp.zeros((ROWS, HEAD), F32)
    row = lax.broadcasted_iota(jnp.int32, (ROWS, HEAD), 0)
    for k in range(heads):
        owner = (me_seq - k) & (heads - 1)
        column = owner * TOKENS + (row & 3)
        gathered = gathered + jnp.where(lane == column, logs[k * ROWS:(k + 1) * ROWS, :], 0.0)
    pick = lax.broadcasted_iota(jnp.int32, log_ref.shape[:1] + (ROWS,), 1) >> 2
    pick = (pick == lax.broadcasted_iota(jnp.int32, pick.shape, 0)).astype(F32)
    log_ref[...] = jnp.dot(pick, gathered, preferred_element_type=F32, precision=lax.Precision.HIGHEST)
    dp_total(total_recv, 2).wait_recv()
    whole32[me_dp] = total_send[...]
    for k in range(1, groups):
        whole32[lax.rem(me_dp + groups - k, groups)] = total_recv[k - 1]
    for d in range(groups):
        up_out[d * up_rows:(d + 1) * up_rows, :] = whole32[d, 0:up_rows, :]

    down_total = seq_copy(lax.rem(me_seq + 1, heads), down_send.at[pl.ds(0, heads - 1)], down_recv, 1)
    down_total.wait_recv()
    share = down_send[me_seq].astype(F32)
    for k in range(heads - 1):
        share = share + down_recv[k].astype(F32)
    share_recv[0] = share.astype(BF16)

    def send_share(k, carry):
        dp_copy(lax.rem(me_dp + k, groups), share_recv.at[0], share_recv.at[k], 3).start()
        return carry

    lax.fori_loop(1, groups, send_share, 0)
    share_total = dp_total(share_recv.at[pl.ds(1, groups - 1)], 3)
    share_total.wait_recv()
    share = jnp.zeros((FOLD, HEAD), F32)
    for d in range(groups):
        share = share + share_recv[lax.rem(me_dp + groups - d, groups)].astype(F32)
    share = share * scale
    turned = pltpu.roll(share, RANK, 1)
    whole = jnp.concatenate(
        [share, turned[:ROWS - FOLD], jnp.zeros((HEAD - ROWS, HEAD), F32)], axis=0
    )
    down_out[...] = whole.T[:RANK, :ROWS]

    dp_total(feat_recv, 0).wait_send()
    dp_total(up_recv, 1).wait_send()
    dp_total(total_recv, 2).wait_send()
    share_total.wait_send()
    partial_total.wait_send()
    down_total.wait_send()


def attend(
    tables, segments, up, query, keys, values, grads, adapter, feat_moving, feat_staying, scale, blocks, groups, heads
):
    total = heads * ROWS
    tile = 4 * ROWS if heads % 4 == 0 else 2 * ROWS
    slots = (groups - 1) * CAP
    inputs = feat_staying.shape[1]
    vmem = pl.BlockSpec(memory_space=pltpu.VMEM)
    up_tile = max(8, RANK // groups)
    folded = (FOLD, HEAD)
    return pl.pallas_call(
        functools.partial(attend_kernel, groups, heads, tile, scale),
        out_shape=(
            jax.ShapeDtypeStruct((RANK, ROWS), F32),
            jax.ShapeDtypeStruct((RANK, HEAD), F32),
            jax.ShapeDtypeStruct((blocks, HEAD), F32),
        ),
        in_specs=[pl.BlockSpec(memory_space=pltpu.SMEM), vmem, pl.BlockSpec(memory_space=pl.ANY)] + [vmem] * 7,
        out_specs=[vmem] * 3,
        scratch_shapes=[
            pltpu.VMEM((total, HEAD), BF16),
            pltpu.VMEM((total, HEAD), BF16),
            pltpu.VMEM((total, 2 * HEAD), BF16),
            pltpu.VMEM((total, 2 * HEAD), BF16),
            pltpu.VMEM((tile, total), F32),
            pltpu.VMEM((tile, total), BF16),
            pltpu.VMEM((total, HEAD), BF16),
            pltpu.VMEM((total, HEAD), F32),
            pltpu.VMEM((RANK, HEAD), BF16),
            pltpu.VMEM(feat_moving.shape, BF16),
            pltpu.VMEM((slots * TOKENS, inputs), F32),
            pltpu.VMEM((heads,) + folded, BF16),
            pltpu.VMEM((heads - 1,) + folded, BF16),
            pltpu.VMEM((LIVE + 1, TOKENS, HEAD), F32),
            pltpu.VMEM(((slots + LIVE) * TOKENS, HEAD), F32),
            pltpu.VMEM((heads,) + folded, BF16),
            pltpu.VMEM((heads - 1,) + folded, BF16),
            pltpu.VMEM((groups, up_tile, HEAD), F32),
            pltpu.VMEM((groups - 1, up_tile, HEAD), F32),
            pltpu.VMEM((up_tile, HEAD), F32),
            pltpu.VMEM((groups - 1, up_tile, HEAD), F32),
            pltpu.VMEM((groups, up_tile, HEAD), F32),
            pltpu.VMEM((groups,) + folded, BF16),
            pltpu.SemaphoreType.DMA,
            pltpu.SemaphoreType.DMA((2,)),
            pltpu.SemaphoreType.DMA((2,)),
            pltpu.SemaphoreType.DMA((4,)),
            pltpu.SemaphoreType.DMA((4,)),
        ],
        compiler_params=pltpu.CompilerParams(
            collective_id=2, has_side_effects=True, vmem_limit_bytes=VMEM_LIMIT
        ),
        name="attend",
    )(tables, segments, up, query, keys, values, grads, adapter, feat_moving, feat_staying)


def per_device(
    features, frozen_query_weight, source_keys, source_values, output_gradient,
    adapter_down_weight, adapter_up_weight, source_block_plan, segments,
):
    groups = lax.axis_size("dp")
    heads = lax.axis_size("seq")
    length = segments.shape[1]
    blocks = source_keys.shape[1]
    tables = block_tables(source_block_plan, groups)
    keys, values, query, grads, adapter, feat_moving, feat_staying = exchange(
        tables, source_keys[0], source_values[0], frozen_query_weight[0], output_gradient[0], features[0],
        adapter_down_weight.T, adapter_up_weight, groups, heads,
    )
    total = heads * ROWS
    scale = 4.0 / math.sqrt(groups * length)
    down, up, logs = attend(
        tables, segments, adapter_up_weight, query.reshape(total, HEAD), keys.reshape(total, HEAD),
        values.reshape(total, HEAD), grads.reshape(total, HEAD), adapter, feat_moving, feat_staying,
        scale, blocks, groups, heads,
    )
    log_norm = logs[:, : TOKENS * heads].reshape(1, 1, length)
    return (down.T, up, log_norm)


def solution(mesh):
    in_specs = (
        P("dp", None, "seq", None),
        P("dp", None, "seq", None),
        P("dp", None, "seq", None),
        P("dp", None, "seq", None),
        P("dp", None, "seq", None),
        P(),
        P(),
        P(),
        P("dp", None),
    )
    out_specs = (P("seq", None), P(None, "seq"), P("dp", "seq", None))
    return jax.shard_map(
        per_device, mesh=mesh, in_specs=in_specs, out_specs=out_specs, check_vma=False
    )
```

```python
import functools
import math

import jax
import jax.numpy as jnp
from jax import lax
from jax.experimental import pallas as pl
from jax.experimental.pallas import tpu as pltpu
from jax.sharding import PartitionSpec as P

CAP = 2
HEAD = 128
RANK = 64
TOKENS = 4
LIVE = 20
ROWS = LIVE * TOKENS
PARTS = 4
FOLD = 48
MESH = pl.DeviceIdType.MESH
BF16 = jnp.bfloat16
F32 = jnp.float32
VMEM_LIMIT = 56 * 1024 * 1024


def tables_kernel(groups, plan_ref, tab_ref):
    group = lax.axis_index("dp")
    blocks = plan_ref.shape[1]
    shift = blocks.bit_length() - 1
    plan = plan_ref[...]
    source, local = plan >> shift, plan & (blocks - 1)
    row = lax.broadcasted_iota(jnp.int32, (groups, blocks), 0)
    place = lax.broadcasted_iota(jnp.int32, (groups, blocks), 1)
    live = place < LIVE
    first = lax.broadcasted_iota(jnp.int32, (blocks, blocks), 0)
    second = lax.broadcasted_iota(jnp.int32, (blocks, blocks), 1)
    match = live & (source == group)
    rank = jnp.dot(match.astype(F32), (first < second).astype(F32), preferred_element_type=F32)

    def column(chosen, value):
        return jnp.sum(jnp.where(chosen, value, 0), axis=1, keepdims=True)

    send = [column(match & (rank == r), local) for r in range(CAP)]
    own = jnp.sum(jnp.where(row == group, plan, 0), axis=0, keepdims=True)
    own_source, own_local = own >> shift, own & (blocks - 1)
    down_column = jnp.sum(jnp.where(first == second, own_source, 0), axis=1, keepdims=True)
    same = (down_column == own_source) & (first < second)
    own_rank = jnp.sum(same.astype(jnp.int32), axis=0, keepdims=True)
    back = [
        LIVE + column(live & (own_source == row) & (own_rank == r), place - LIVE) for r in range(CAP)
    ]
    stays = own_source == group
    distance = (group - own_source + groups) & (groups - 1)
    take = jnp.where(stays, 0, (distance - 1) * CAP + own_rank)
    tab_ref[...] = jnp.zeros_like(tab_ref)
    for at, part in enumerate(send + back):
        tab_ref[0:groups, at:at + 1] = part
    tab_ref[groups:groups + 1, 0:blocks] = take
    tab_ref[groups + 1:groups + 2, 0:blocks] = jnp.where(stays, own_local, 0)
    tab_ref[groups + 2:groups + 3, 0:blocks] = stays.astype(jnp.int32)


def block_tables(plan, groups):
    vmem = pl.BlockSpec(memory_space=pltpu.VMEM)
    return pl.pallas_call(
        functools.partial(tables_kernel, groups),
        out_shape=jax.ShapeDtypeStruct((24, HEAD), jnp.int32),
        in_specs=[vmem],
        out_specs=vmem,
        name="tables",
    )(plan)


def greet_all(groups, heads, me_dp, me_seq):
    barrier = pltpu.get_barrier_semaphore()

    def greet_dp(k, carry):
        pl.semaphore_signal(
            barrier, inc=1, device_id=(lax.rem(me_dp + k, groups), me_seq), device_id_type=MESH
        )
        return carry

    def greet_seq(k, carry):
        pl.semaphore_signal(
            barrier, inc=1, device_id=(me_dp, lax.rem(me_seq + k, heads)), device_id_type=MESH
        )
        return carry

    lax.fori_loop(1, groups, greet_dp, 0)
    lax.fori_loop(1, heads, greet_seq, 0)
    return barrier


def whole_kernel(
    groups, heads, parts, scale, tab, segments_ref, down_ref, up_ref, keys_in, values_in, base_in, grad_in, feat_in,
    down_out, up_out, log_ref,
    *scratch,
):
    keys_pool, values_pool, query_pool = (scratch[n * parts:(n + 1) * parts] for n in range(3))
    (
        adapter_pool,
        keys_here, values_here, query_here, adapter_here, grad_buf, feat_buf,
        keys_send, values_send, query_send, adapter_send,
        keys_stage, values_stage, query_stage, grad_stage, adapter_stage, rows32, feat32, up32, adapter32,
        keys_got, values_got, query_got, grad_got, adapter_got, feat_moving, feat_staying,
        key_max, key_sum, value_sum, value_neg, scores, probs, dquery, logs, up_head,
        feat_recv, partial_send, partial_recv, blocks32, pieces, down_send, down_recv,
        up_send, up_recv, total_send, total_recv, whole32, share_recv,
        up_sem, load_sem, own_sem, z_send, z_recv, s_send, s_recv,
    ) = scratch[3 * parts:]
    me_dp = lax.axis_index("dp")
    me_seq = lax.axis_index("seq")
    slots = (groups - 1) * CAP
    blocks = keys_in.shape[0]
    total = heads * ROWS
    tile = total // parts
    step = 256 if total % 256 == 0 else total
    per_tile = tile // ROWS
    up_rows = RANK // groups
    seq_base = 5
    dp_base = 3 * parts + 1
    scaling = 1.0 / math.sqrt(HEAD)
    to_exp2 = scaling * math.log2(math.e)
    nt = (((1,), (1,)), ((), ()))
    tn = (((0,), (0,)), ((), ()))
    zero = jnp.zeros((), BF16)
    per_part = heads // parts

    def head_of(part, c):
        return c * parts + ((part - c) & (parts - 1))

    def slot_source(i):
        return tab[lax.rem(me_dp + 1 + i // CAP, groups), i % CAP]

    loads = [
        pltpu.make_async_copy(keys_in, keys_here, load_sem.at[0]),
        pltpu.make_async_copy(base_in, query_here, load_sem.at[1]),
        pltpu.make_async_copy(feat_in, feat_buf, load_sem.at[2]),
        pltpu.make_async_copy(grad_in, grad_buf, load_sem.at[3]),
        pltpu.make_async_copy(values_in, values_here, load_sem.at[4]),
    ]
    for copy in loads:
        copy.start()
    barrier = greet_all(groups, heads, me_dp, me_seq)
    up_copy = pltpu.make_async_copy(
        up_ref.at[:, pl.ds(pl.multiple_of(me_seq * HEAD, HEAD), HEAD)], up_head, up_sem
    )
    up_copy.start()

    def pack(here, send):
        for i in range(slots):
            block = here[slot_source(i)]
            for part in range(parts):
                for c in range(per_part):
                    h = head_of(part, c)
                    send[part, i, :, c * HEAD:(c + 1) * HEAD] = block[:, h * HEAD:(h + 1) * HEAD]

    def send_dp(send, pool, index):
        def one(k, carry):
            pltpu.make_async_remote_copy(
                src_ref=send.at[pl.ds((k - 1) * CAP, CAP)],
                dst_ref=pool.at[pl.ds((k - 1) * CAP, CAP)],
                send_sem=z_send.at[index],
                recv_sem=z_recv.at[index],
                device_id=(lax.rem(me_dp + k, groups), me_seq),
                device_id_type=MESH,
            ).start()
            return carry

        lax.fori_loop(1, groups, one, 0)

    def dp_part(send, pool, index):
        return pltpu.make_async_remote_copy(
            src_ref=send,
            dst_ref=pool,
            send_sem=z_send.at[index],
            recv_sem=z_recv.at[index],
            device_id=(lax.rem(me_dp + 1, groups), me_seq),
            device_id_type=MESH,
        )

    def send_seq(src, out, index, peer):
        @pl.when(peer != me_seq)
        def _():
            pltpu.make_async_remote_copy(
                src_ref=src,
                dst_ref=out.at[lax.rem(peer + heads - me_seq, heads)],
                send_sem=s_send.at[index],
                recv_sem=s_recv.at[index],
                device_id=(me_dp, peer),
                device_id_type=MESH,
            ).start()

        @pl.when(peer == me_seq)
        def _():
            pltpu.make_async_copy(src, out.at[0], own_sem.at[index]).start()

    def send_part(stage, out, index, part):
        def one(step, carry):
            c = lax.rem(step + 1 + me_seq // parts, per_part)
            peer = head_of(part, c)
            send_seq(stage.at[peer], out, index, peer)
            return carry

        lax.fori_loop(0, per_part, one, 0)

    def seq_total(out, index):
        return pltpu.make_async_remote_copy(
            src_ref=out.at[pl.ds(1, heads - 1)],
            dst_ref=out.at[pl.ds(1, heads - 1)],
            send_sem=s_send.at[index],
            recv_sem=s_recv.at[index],
            device_id=(me_dp, lax.rem(me_seq + 1, heads)),
            device_id_type=MESH,
        )

    def dest_block(moved, kept, j):
        return jnp.where(tab[groups + 2, j] == 1, kept.astype(F32), moved.astype(F32))

    def pass_on(pool, here, stage, out, index, part):
        for j in range(LIVE):
            kept = here[tab[groups + 1, j]]
            kept = jnp.concatenate(
                [kept[:, h * HEAD:(h + 1) * HEAD] for h in [head_of(part, c) for c in range(per_part)]], axis=1
            )
            rows32[j * TOKENS:(j + 1) * TOKENS, : per_part * HEAD] = dest_block(
                pool[part][tab[groups, j]], kept, j
            )
        for c in range(per_part):
            stage[head_of(part, c)] = rows32[:, c * HEAD:(c + 1) * HEAD].astype(BF16)
        send_part(stage, out, index, part)

    loads[0].wait()
    pack(keys_here, keys_send)
    pl.semaphore_wait(barrier, groups + heads - 2)
    for part in range(parts):
        send_dp(keys_send.at[part], keys_pool[part], part)

    loads[3].wait()
    for j in range(LIVE):
        rows32[j * TOKENS:(j + 1) * TOKENS, :] = grad_buf[j].astype(F32)
    for h in range(heads):
        grad_stage[h] = rows32[:, h * HEAD:(h + 1) * HEAD].astype(BF16)
    for part in range(parts):
        send_part(grad_stage, grad_got, 3, part)

    loads[1].wait()
    loads[2].wait()
    for b in range(blocks):
        feat32[b * TOKENS:(b + 1) * TOKENS, :] = feat_buf[b].astype(F32)
    features = feat32[: blocks * TOKENS, :].astype(BF16)
    adapter = lax.dot_general(features, down_ref[...], nt, preferred_element_type=F32).astype(BF16)
    adapter32[: blocks * TOKENS, :] = jnp.concatenate([adapter, adapter], axis=1).astype(F32)
    up32[...] = jnp.dot(adapter, up_ref[...], preferred_element_type=F32)
    for b in range(blocks):
        query_here[b] = (query_here[b].astype(F32) + up32[b * TOKENS:(b + 1) * TOKENS, :]).astype(BF16)
        adapter_here[b] = adapter32[b * TOKENS:(b + 1) * TOKENS, :].astype(BF16)
    pack(query_here, query_send)
    for i in range(slots):
        adapter_send[i] = adapter_here[slot_source(i)]
    send_dp(adapter_send, adapter_pool, 3 * parts)
    for part in range(parts):
        send_dp(query_send.at[part], query_pool[part], parts + part)
    loads[4].wait()
    pack(values_here, values_send)
    for part in range(parts):
        send_dp(values_send.at[part], values_pool[part], 2 * parts + part)

    for i in range(slots):
        feat32[i * TOKENS:(i + 1) * TOKENS, :] = feat_buf[slot_source(i)].astype(F32)
    for k in range(groups - 1):
        feat_moving[k] = feat32[k * CAP * TOKENS:(k + 1) * CAP * TOKENS, :].astype(BF16)
    for j in range(LIVE):
        feat32[j * TOKENS:(j + 1) * TOKENS, :] = feat_buf[tab[groups + 1, j]].astype(F32)
    feat_staying[...] = feat32[:ROWS, :].astype(BF16)

    def take_part(send, pool, here, stage, got, index, order, part):
        dp_part(send.at[part], pool[part], order * parts + part).wait_recv()
        pass_on(pool, here, stage, got, index, part)

    def position(first, rows):
        token = first + lax.broadcasted_iota(jnp.int32, (rows, HEAD), 0)
        part = (token * 52429) >> 22
        rest = token - part * ROWS
        owner = (me_seq - part) & (heads - 1)
        return (rest >> 2) * (TOKENS * heads) + owner * TOKENS + (rest & 3)

    live_count = jnp.sum((segments_ref[...] < 1).astype(jnp.int32), axis=1, keepdims=True)
    lane80 = lax.broadcasted_iota(jnp.int32, (ROWS, HEAD), 1)
    for part in range(parts):
        take_part(keys_send, keys_pool, keys_here, keys_stage, keys_got, 0, 0, part)
    dp_part(adapter_send, adapter_pool, 3 * parts).wait_recv()
    adapter32[...] = jnp.zeros_like(adapter32)
    for j in range(LIVE):
        adapter32[j * TOKENS:(j + 1) * TOKENS, :] = dest_block(
            adapter_pool[tab[groups, j]], adapter_here[tab[groups + 1, j]], j
        )
    lane = lax.broadcasted_iota(jnp.int32, (FOLD, HEAD), 1)
    adapter_stage[...] = jnp.where(
        lane < RANK, adapter32[0:FOLD, :], adapter32[FOLD:2 * FOLD, :]
    ).astype(BF16)

    def spread(k, carry):
        send_seq(adapter_stage, adapter_got, 4, lax.rem(me_seq + k, heads))
        return carry

    lax.fori_loop(0, heads, spread, 0)
    for k in range(heads):
        at = slice(k * ROWS, (k + 1) * ROWS)
        live = position(k * ROWS, ROWS) < live_count
        value_sum[at, HEAD:] = jnp.where(live, 1.0, 0.0).astype(BF16)
        value_neg[at, HEAD:] = jnp.where(lane80 < 3, -1.0, 0.0).astype(BF16)
    for part in range(parts):
        if part == parts // 2:
            seq_total(keys_got, 0).wait_recv()
            pltpu.make_async_copy(keys_stage.at[0], keys_got.at[0], own_sem.at[0]).wait()
            filler = keys_got[me_seq][0:1, :]
            for k in range(heads):
                at = slice(k * ROWS, (k + 1) * ROWS)
                live = position(k * ROWS, ROWS) < live_count
                rows = keys_got[k]
                key_max[at, :] = jnp.where(live, rows, filler)
                key_sum[at, :] = jnp.where(live, rows, zero)
        take_part(query_send, query_pool, query_here, query_stage, query_got, 2, 1, part)

    tops = []

    def score_tile(t):
        query = query_got[t * per_tile:(t + 1) * per_tile].reshape(tile, HEAD)
        top = None
        for c in range(0, total, step):
            part_scores = lax.dot_general(query, key_max[c:c + step, :], nt, preferred_element_type=F32)
            scores[:, c:c + step] = part_scores
            for b in range(0, step, HEAD):
                piece = part_scores[:, b:b + HEAD]
                top = piece if top is None or piece.shape != top.shape else jnp.maximum(top, piece)
        top = jnp.max(top if step % HEAD == 0 else scores[...], axis=1, keepdims=True)
        for c in range(0, total, step):
            probs[t * tile:(t + 1) * tile, c:c + step] = jnp.exp2(
                (scores[:, c:c + step] - top) * to_exp2
            ).astype(BF16)
        logs[t * tile:(t + 1) * tile, :] = jnp.broadcast_to(top * scaling, (tile, HEAD))

    def dp_copy(k, src, dst, index):
        return pltpu.make_async_remote_copy(
            src_ref=src, dst_ref=dst, send_sem=z_send.at[dp_base + index], recv_sem=z_recv.at[dp_base + index],
            device_id=(k, me_seq), device_id_type=MESH,
        )

    def seq_copy(k, src, dst, index):
        return pltpu.make_async_remote_copy(
            src_ref=src, dst_ref=dst, send_sem=s_send.at[seq_base + index], recv_sem=s_recv.at[seq_base + index],
            device_id=(me_dp, k), device_id_type=MESH,
        )

    def send_features(k, carry):
        dp_copy(lax.rem(me_dp + k, groups), feat_moving.at[k - 1], feat_recv.at[k - 1], 0).start()
        return carry

    for part in range(parts):
        take_part(values_send, values_pool, values_here, values_stage, values_got, 1, 2, part)
        if part == 0:
            seq_total(query_got, 2).wait_recv()
            pltpu.make_async_copy(query_stage.at[0], query_got.at[0], own_sem.at[2]).wait()
        if part == parts - 1:
            lax.fori_loop(1, groups, send_features, 0)
        score_tile(part)

    up_copy.wait()
    up = up_head[...]
    nothing = jnp.zeros((RANK, HEAD), BF16)
    to_low = jnp.concatenate([up, nothing], axis=0)
    to_high = jnp.concatenate([nothing, up], axis=0)
    filling = jnp.zeros((2 * FOLD - ROWS, HEAD), BF16)
    lanes = lax.broadcasted_iota(jnp.int32, (tile, HEAD), 1)

    seq_total(grad_got, 3).wait_recv()
    pltpu.make_async_copy(grad_stage.at[0], grad_got.at[0], own_sem.at[3]).wait()
    seq_total(values_got, 1).wait_recv()
    pltpu.make_async_copy(values_stage.at[0], values_got.at[0], own_sem.at[1]).wait()
    for k in range(heads):
        at = slice(k * ROWS, (k + 1) * ROWS)
        value = jnp.where(position(k * ROWS, ROWS) < live_count, values_got[k], zero)
        value_sum[at, 0:HEAD] = value
        value_neg[at, 0:HEAD] = value

    state = [dict() for _ in range(parts)]

    def attend_step(t, c):
        own = state[t]
        add = jnp.dot(
            probs[t * tile:(t + 1) * tile, c:c + step], value_sum[c:c + step, :], preferred_element_type=F32
        )
        own["sum"] = add if c == 0 else own["sum"] + add
        if c + step == total:
            norm = own["sum"][:, HEAD:]
            inverse = 1.0 / norm
            grad = grad_got[t * per_tile:(t + 1) * per_tile].reshape(tile, HEAD)
            delta = jnp.sum(grad.astype(F32) * own["sum"][:, :HEAD], axis=1, keepdims=True) * inverse
            high = delta.astype(BF16)
            middle = (delta - high.astype(F32)).astype(BF16)
            low = (delta - high.astype(F32) - middle.astype(F32)).astype(BF16)
            split = jnp.where(lanes == 0, high, jnp.where(lanes == 1, middle, jnp.where(lanes == 2, low, zero)))
            own["wide"] = jnp.concatenate([grad, split], axis=1)
            own["factor"] = inverse * scaling
            at = slice(t * tile, (t + 1) * tile)
            own["live"] = position(t * tile, tile) < live_count
            logs[at, :] = jnp.where(own["live"], logs[at, :] + jnp.log(norm), 0.0)

    def gradient_step(t, c):
        own = state[t]
        dprob = lax.dot_general(own["wide"], value_neg[c:c + step, :], nt, preferred_element_type=F32)
        dscore = (probs[t * tile:(t + 1) * tile, c:c + step].astype(F32) * dprob).astype(BF16)
        add = jnp.dot(dscore, key_sum[c:c + step, :], preferred_element_type=F32)
        own["grad"] = add if c == 0 else own["grad"] + add
        if c + step == total:
            result = jnp.where(own["live"], own["grad"] * own["factor"], 0.0).astype(BF16)
            dquery[t * tile:(t + 1) * tile, :] = result
            for i in range(per_tile):
                k = t * per_tile + i
                first_part = result[i * ROWS:i * ROWS + FOLD]
                second_part = jnp.concatenate([result[i * ROWS + FOLD:(i + 1) * ROWS], filling], axis=0)
                partial_send[k] = (
                    lax.dot_general(first_part, to_low, nt, preferred_element_type=F32)
                    + lax.dot_general(second_part, to_high, nt, preferred_element_type=F32)
                ).astype(BF16)
                if k > 0:
                    seq_copy(
                        lax.rem(me_seq + heads - k, heads), partial_send.at[k], partial_recv.at[k - 1], 0
                    ).start()

    for t in range(parts + 1):
        for c in range(0, total, step):
            if t < parts:
                attend_step(t, c)
            if t > 0:
                gradient_step(t - 1, c)

    seq_total(adapter_got, 4).wait_recv()
    pltpu.make_async_copy(adapter_stage, adapter_got.at[0], own_sem.at[4]).wait()
    up_total = jnp.zeros((RANK, HEAD), F32)
    for k in range(heads):
        first_part = dquery[k * ROWS:k * ROWS + FOLD, :]
        second_part = jnp.concatenate([dquery[k * ROWS + FOLD:(k + 1) * ROWS, :], filling], axis=0)
        folded = adapter_got[k]
        up_total = up_total + lax.dot_general(folded, first_part, tn, preferred_element_type=F32)[:RANK]
        up_total = up_total + lax.dot_general(folded, second_part, tn, preferred_element_type=F32)[RANK:]
    up_send[...] = jnp.zeros_like(up_send)
    for d in range(groups):
        up_send[d, 0:up_rows, :] = up_total[d * up_rows:(d + 1) * up_rows, :]

    def send_up(k, carry):
        peer = lax.rem(me_dp + k, groups)
        dp_copy(peer, up_send.at[peer], up_recv.at[k - 1], 1).start()
        return carry

    lax.fori_loop(1, groups, send_up, 0)

    def dp_total(like, index):
        return dp_copy(lax.rem(me_dp + 1, groups), like, like, index)

    dp_total(feat_recv, 0).wait_recv()
    for k in range(groups - 1):
        feat32[k * CAP * TOKENS:(k + 1) * CAP * TOKENS, :] = feat_recv[k].astype(F32)
    moved_rows = feat32[: slots * TOKENS, :].astype(BF16)

    partial_total = seq_copy(lax.rem(me_seq + 1, heads), partial_send.at[pl.ds(1, heads - 1)], partial_recv, 0)
    partial_total.wait_recv()
    folded = partial_send[0].astype(F32)
    for k in range(heads - 1):
        folded = folded + partial_recv[k].astype(F32)
    turned = pltpu.roll(folded, RANK, 1)
    for j in range(LIVE):
        row = j * TOKENS
        half = folded if row < FOLD else turned
        row = row if row < FOLD else row - FOLD
        blocks32[j] = half[row:row + TOKENS, :]
    blocks32[LIVE] = jnp.zeros((TOKENS, HEAD), F32)
    for k in range(1, groups):
        origin = lax.rem(me_dp + groups - k, groups)
        for r in range(CAP):
            row = ((k - 1) * CAP + r) * TOKENS
            pieces[row:row + TOKENS, :] = blocks32[tab[origin, CAP + r]]
    for j in range(LIVE):
        stays = tab[groups + 2, j].astype(F32)
        pieces[(slots + j) * TOKENS:(slots + j + 1) * TOKENS, :] = blocks32[j] * stays
    own_lane = lax.broadcasted_iota(jnp.int32, pieces.shape, 1)
    grads = pieces[...]
    doubled = jnp.where(own_lane < RANK, grads, pltpu.roll(grads, RANK, 1)).astype(BF16)
    down = lax.dot_general(doubled[:slots * TOKENS], moved_rows, tn, preferred_element_type=F32)
    down = down + lax.dot_general(doubled[slots * TOKENS:], feat_staying[...], tn, preferred_element_type=F32)
    down = down.T
    fold_lane = lax.broadcasted_iota(jnp.int32, (FOLD, HEAD), 1)
    for h in range(heads):
        first = down[h * ROWS:h * ROWS + FOLD, :]
        second = jnp.concatenate(
            [down[h * ROWS + FOLD:(h + 1) * ROWS, :], jnp.zeros((2 * FOLD - ROWS, HEAD), F32)], axis=0
        )
        down_send[h] = jnp.where(fold_lane < RANK, first, second).astype(BF16)

    def send_down(k, carry):
        peer = lax.rem(me_seq + k, heads)
        seq_copy(peer, down_send.at[peer], down_recv.at[k - 1], 1).start()
        return carry

    lax.fori_loop(1, heads, send_down, 0)

    dp_total(up_recv, 1).wait_recv()
    up_sum = up_send[me_dp]
    for k in range(groups - 1):
        up_sum = up_sum + up_recv[k]
    total_send[...] = up_sum * scale

    def send_total(k, carry):
        dp_copy(lax.rem(me_dp + k, groups), total_send, total_recv.at[k - 1], 2).start()
        return carry

    lax.fori_loop(1, groups, send_total, 0)
    gathered = jnp.zeros((ROWS, HEAD), F32)
    row = lax.broadcasted_iota(jnp.int32, (ROWS, HEAD), 0)
    for k in range(heads):
        owner = (me_seq - k) & (heads - 1)
        column = owner * TOKENS + (row & 3)
        gathered = gathered + jnp.where(lane80 == column, logs[k * ROWS:(k + 1) * ROWS, :], 0.0)
    pick = lax.broadcasted_iota(jnp.int32, log_ref.shape[:1] + (ROWS,), 1) >> 2
    pick = (pick == lax.broadcasted_iota(jnp.int32, pick.shape, 0)).astype(F32)
    log_ref[...] = jnp.dot(pick, gathered, preferred_element_type=F32, precision=lax.Precision.HIGHEST)
    dp_total(total_recv, 2).wait_recv()
    whole32[me_dp] = total_send[...]
    for k in range(1, groups):
        whole32[lax.rem(me_dp + groups - k, groups)] = total_recv[k - 1]
    for d in range(groups):
        up_out[d * up_rows:(d + 1) * up_rows, :] = whole32[d, 0:up_rows, :]

    down_total = seq_copy(lax.rem(me_seq + 1, heads), down_send.at[pl.ds(0, heads - 1)], down_recv, 1)
    down_total.wait_recv()
    share = down_send[me_seq].astype(F32)
    for k in range(heads - 1):
        share = share + down_recv[k].astype(F32)
    share_recv[0] = share.astype(BF16)

    def send_share(k, carry):
        dp_copy(lax.rem(me_dp + k, groups), share_recv.at[0], share_recv.at[k], 3).start()
        return carry

    lax.fori_loop(1, groups, send_share, 0)
    share_total = dp_total(share_recv.at[pl.ds(1, groups - 1)], 3)
    share_total.wait_recv()
    share = jnp.zeros((FOLD, HEAD), F32)
    for d in range(groups):
        share = share + share_recv[lax.rem(me_dp + groups - d, groups)].astype(F32)
    share = share * scale
    turned = pltpu.roll(share, RANK, 1)
    whole = jnp.concatenate(
        [share, turned[:ROWS - FOLD], jnp.zeros((HEAD - ROWS, HEAD), F32)], axis=0
    )
    down_out[...] = whole.T[:RANK, :ROWS]

    dp_total(feat_recv, 0).wait_send()
    dp_total(up_recv, 1).wait_send()
    dp_total(total_recv, 2).wait_send()
    share_total.wait_send()
    partial_total.wait_send()
    down_total.wait_send()
    for part in range(parts):
        dp_part(keys_send.at[part], keys_pool[part], part).wait_send()
        dp_part(query_send.at[part], query_pool[part], parts + part).wait_send()
        dp_part(values_send.at[part], values_pool[part], 2 * parts + part).wait_send()
    dp_part(adapter_send, adapter_pool, 3 * parts).wait_send()
    for index, got in enumerate((keys_got, values_got, query_got, grad_got, adapter_got)):
        seq_total(got, index).wait_send()


def whole(tables, segments, down_t, up, keys, values, base, grads, features, scale, groups, heads):
    blocks = keys.shape[0]
    slots = (groups - 1) * CAP
    width = heads * HEAD
    total = heads * ROWS
    parts = min(PARTS, heads)
    inputs = features.shape[2]
    vmem = pl.BlockSpec(memory_space=pltpu.VMEM)
    hbm = pl.BlockSpec(memory_space=pl.ANY)
    up_tile = max(8, RANK // groups)

    def array(*shape, dtype=BF16):
        return pltpu.VMEM(shape, dtype)

    def numbers(*shape):
        return pltpu.VMEM(shape, F32)

    arriving = array(slots, TOKENS, width // parts)
    moving = array(parts, slots, TOKENS, width // parts)
    here = array(blocks, TOKENS, width)
    chunks = array(heads, ROWS, HEAD)
    folded = array(heads, FOLD, HEAD)
    received = array(heads - 1, FOLD, HEAD)
    return pl.pallas_call(
        functools.partial(whole_kernel, groups, heads, parts, scale),
        out_shape=(
            jax.ShapeDtypeStruct((RANK, ROWS), F32),
            jax.ShapeDtypeStruct((RANK, HEAD), F32),
            jax.ShapeDtypeStruct((blocks, HEAD), F32),
        ),
        in_specs=[pl.BlockSpec(memory_space=pltpu.SMEM)] + [vmem] * 3 + [hbm] * 5,
        out_specs=[vmem] * 3,
        scratch_shapes=[arriving] * (3 * parts) + [
            array(slots, TOKENS, HEAD),
            here, here, here, array(blocks, TOKENS, HEAD), here, array(blocks, TOKENS, inputs),
            moving, moving, moving, array(slots, TOKENS, HEAD),
            chunks, chunks, chunks, chunks, array(FOLD, HEAD),
            numbers(ROWS, width),
            numbers(max(slots, blocks) * TOKENS, inputs),
            numbers(blocks * TOKENS, width),
            numbers(max(blocks * TOKENS, 2 * FOLD), HEAD),
            chunks, chunks, chunks, chunks, folded,
            array(groups - 1, CAP * TOKENS, inputs), array(ROWS, inputs),
            array(total, HEAD), array(total, HEAD), array(total, 2 * HEAD), array(total, 2 * HEAD),
            numbers(total // parts, total), array(total, total), array(total, HEAD), numbers(total, HEAD),
            array(RANK, HEAD),
            array(groups - 1, CAP * TOKENS, inputs),
            folded, received,
            numbers(LIVE + 1, TOKENS, HEAD), numbers((slots + LIVE) * TOKENS, HEAD),
            folded, received,
            numbers(groups, up_tile, HEAD), numbers(groups - 1, up_tile, HEAD),
            numbers(up_tile, HEAD), numbers(groups - 1, up_tile, HEAD), numbers(groups, up_tile, HEAD),
            array(groups, FOLD, HEAD),
            pltpu.SemaphoreType.DMA,
            pltpu.SemaphoreType.DMA((5,)),
            pltpu.SemaphoreType.DMA((5,)),
            pltpu.SemaphoreType.DMA((3 * parts + 5,)),
            pltpu.SemaphoreType.DMA((3 * parts + 5,)),
            pltpu.SemaphoreType.DMA((7,)),
            pltpu.SemaphoreType.DMA((7,)),
        ],
        compiler_params=pltpu.CompilerParams(
            collective_id=1, has_side_effects=True, vmem_limit_bytes=VMEM_LIMIT
        ),
        name="whole",
    )(tables, segments, down_t, up, keys, values, base, grads, features)


def per_device(
    features, frozen_query_weight, source_keys, source_values, output_gradient,
    adapter_down_weight, adapter_up_weight, source_block_plan, segments,
):
    groups = lax.axis_size("dp")
    heads = lax.axis_size("seq")
    length = segments.shape[1]
    tables = block_tables(source_block_plan, groups)
    scale = 4.0 / math.sqrt(groups * length)
    down, up, logs = whole(
        tables, segments, adapter_down_weight.T, adapter_up_weight, source_keys[0], source_values[0],
        frozen_query_weight[0], output_gradient[0], features[0], scale, groups, heads,
    )
    log_norm = logs[:, : TOKENS * heads].reshape(1, 1, length)
    return (down.T, up, log_norm)


def solution(mesh):
    in_specs = (
        P("dp", None, "seq", None),
        P("dp", None, "seq", None),
        P("dp", None, "seq", None),
        P("dp", None, "seq", None),
        P("dp", None, "seq", None),
        P(),
        P(),
        P(),
        P("dp", None),
    )
    out_specs = (P("seq", None), P(None, "seq"), P("dp", "seq", None))
    return jax.shard_map(
        per_device, mesh=mesh, in_specs=in_specs, out_specs=out_specs, check_vma=False
    )
```

```python
import functools
import math

import jax
import jax.numpy as jnp
from jax import lax
from jax.experimental import pallas as pl
from jax.experimental.pallas import tpu as pltpu
from jax.sharding import PartitionSpec as P

CAP = 2
HEAD = 128
RANK = 64
TOKENS = 4
LIVE = 20
ROWS = LIVE * TOKENS
PARTS = 4
FOLD = 48
MESH = pl.DeviceIdType.MESH
BF16 = jnp.bfloat16
F32 = jnp.float32
VMEM_LIMIT = 56 * 1024 * 1024


def tables_kernel(groups, plan_ref, tab_ref):
    group = lax.axis_index("dp")
    blocks = plan_ref.shape[1]
    shift = blocks.bit_length() - 1
    plan = plan_ref[...]
    source, local = plan >> shift, plan & (blocks - 1)
    row = lax.broadcasted_iota(jnp.int32, (groups, blocks), 0)
    place = lax.broadcasted_iota(jnp.int32, (groups, blocks), 1)
    live = place < LIVE
    first = lax.broadcasted_iota(jnp.int32, (blocks, blocks), 0)
    second = lax.broadcasted_iota(jnp.int32, (blocks, blocks), 1)
    match = live & (source == group)
    rank = jnp.dot(match.astype(F32), (first < second).astype(F32), preferred_element_type=F32)

    def column(chosen, value):
        return jnp.sum(jnp.where(chosen, value, 0), axis=1, keepdims=True)

    send = [column(match & (rank == r), local) for r in range(CAP)]
    own = jnp.sum(jnp.where(row == group, plan, 0), axis=0, keepdims=True)
    own_source, own_local = own >> shift, own & (blocks - 1)
    down_column = jnp.sum(jnp.where(first == second, own_source, 0), axis=1, keepdims=True)
    same = (down_column == own_source) & (first < second)
    own_rank = jnp.sum(same.astype(jnp.int32), axis=0, keepdims=True)
    back = [
        LIVE + column(live & (own_source == row) & (own_rank == r), place - LIVE) for r in range(CAP)
    ]
    stays = own_source == group
    distance = (group - own_source + groups) & (groups - 1)
    take = jnp.where(stays, 0, (distance - 1) * CAP + own_rank)
    tab_ref[...] = jnp.zeros_like(tab_ref)
    for at, part in enumerate(send + back):
        tab_ref[0:groups, at:at + 1] = part
    tab_ref[groups:groups + 1, 0:blocks] = take
    tab_ref[groups + 1:groups + 2, 0:blocks] = jnp.where(stays, own_local, 0)
    tab_ref[groups + 2:groups + 3, 0:blocks] = stays.astype(jnp.int32)


def block_tables(plan, groups):
    vmem = pl.BlockSpec(memory_space=pltpu.VMEM)
    return pl.pallas_call(
        functools.partial(tables_kernel, groups),
        out_shape=jax.ShapeDtypeStruct((24, HEAD), jnp.int32),
        in_specs=[vmem],
        out_specs=vmem,
        name="tables",
    )(plan)


def greet_all(groups, heads, me_dp, me_seq):
    barrier = pltpu.get_barrier_semaphore()

    def greet_dp(k, carry):
        pl.semaphore_signal(
            barrier, inc=1, device_id=(lax.rem(me_dp + k, groups), me_seq), device_id_type=MESH
        )
        return carry

    def greet_seq(k, carry):
        pl.semaphore_signal(
            barrier, inc=1, device_id=(me_dp, lax.rem(me_seq + k, heads)), device_id_type=MESH
        )
        return carry

    lax.fori_loop(1, groups, greet_dp, 0)
    lax.fori_loop(1, heads, greet_seq, 0)
    return barrier


def seq_shape(heads):
    across = 4 if heads >= 8 else heads // 2
    return across, heads // across


def whole_kernel(
    groups, heads, parts, scale, tab, segments_ref, down_ref, up_ref, keys_in, values_in, base_in, grad_in, feat_in,
    down_out, up_out, log_ref,
    *scratch,
):
    keys_pool, values_pool, query_pool = (scratch[n * parts:(n + 1) * parts] for n in range(3))
    (
        adapter_pool,
        keys_here, values_here, query_here, adapter_here, grad_buf, feat_buf,
        keys_send, values_send, query_send, adapter_send,
        keys_stage, values_stage, query_stage, grad_stage, adapter_stage, rows32, feat32, up32, adapter32,
        keys_got, values_got, query_got, grad_got, adapter_got, feat_moving, feat_turned,
        key_max, key_sum, value_sum, value_neg, scores, probs, dquery, logs, up_head,
        feat_recv, partial_send, partial_recv, blocks32, pieces, down_send, down_x, down_row, down_y,
        up_send, up_recv, total_send, total_recv, whole32, share_recv,
        up_sem, load_sem, own_sem, z_send, z_recv, s_send, s_recv,
    ) = scratch[3 * parts:]
    me_dp = lax.axis_index("dp")
    me_seq = lax.axis_index("seq")
    slots = (groups - 1) * CAP
    blocks = keys_in.shape[0]
    total = heads * ROWS
    tiles = min(4, heads)
    tile = total // tiles
    step = 256 if total % 256 == 0 else total
    per_tile = tile // ROWS
    stay_row = feat32.shape[0] - HEAD
    up_rows = RANK // groups
    seq_base = 5
    rows_x, rows_y = seq_shape(heads)
    dp_base = 3 * parts + 1
    scaling = 1.0 / math.sqrt(HEAD)
    to_exp2 = scaling * math.log2(math.e)
    nt = (((1,), (1,)), ((), ()))
    tn = (((0,), (0,)), ((), ()))
    zero = jnp.zeros((), BF16)
    per_part = heads // parts

    def head_of(part, c):
        return c * parts + ((part - c) & (parts - 1))

    def slot_source(i):
        return tab[lax.rem(me_dp + 1 + i // CAP, groups), i % CAP]

    loads = [
        pltpu.make_async_copy(keys_in, keys_here, load_sem.at[0]),
        pltpu.make_async_copy(base_in, query_here, load_sem.at[1]),
        pltpu.make_async_copy(feat_in, feat_buf, load_sem.at[2]),
        pltpu.make_async_copy(grad_in, grad_buf, load_sem.at[3]),
        pltpu.make_async_copy(values_in, values_here, load_sem.at[4]),
    ]
    for copy in loads:
        copy.start()
    barrier = greet_all(groups, heads, me_dp, me_seq)
    up_copy = pltpu.make_async_copy(
        up_ref.at[:, pl.ds(pl.multiple_of(me_seq * HEAD, HEAD), HEAD)], up_head, up_sem
    )
    up_copy.start()

    def pack(here, send, part):
        for i in range(slots):
            block = slot_source(i)
            for c in range(per_part):
                h = head_of(part, c)
                send[part, i, :, c * HEAD:(c + 1) * HEAD] = here[block, :, h * HEAD:(h + 1) * HEAD]

    def send_dp(send, pool, index):
        def one(k, carry):
            pltpu.make_async_remote_copy(
                src_ref=send.at[pl.ds((k - 1) * CAP, CAP)],
                dst_ref=pool.at[pl.ds((k - 1) * CAP, CAP)],
                send_sem=z_send.at[index],
                recv_sem=z_recv.at[index],
                device_id=(lax.rem(me_dp + k, groups), me_seq),
                device_id_type=MESH,
            ).start()
            return carry

        lax.fori_loop(1, groups, one, 0)

    def dp_part(send, pool, index):
        return pltpu.make_async_remote_copy(
            src_ref=send,
            dst_ref=pool,
            send_sem=z_send.at[index],
            recv_sem=z_recv.at[index],
            device_id=(lax.rem(me_dp + 1, groups), me_seq),
            device_id_type=MESH,
        )

    def send_seq(src, out, index, peer):
        @pl.when(peer != me_seq)
        def _():
            pltpu.make_async_remote_copy(
                src_ref=src,
                dst_ref=out.at[lax.rem(peer + heads - me_seq, heads)],
                send_sem=s_send.at[index],
                recv_sem=s_recv.at[index],
                device_id=(me_dp, peer),
                device_id_type=MESH,
            ).start()

        @pl.when(peer == me_seq)
        def _():
            pltpu.make_async_copy(src, out.at[0], own_sem.at[index]).start()

    def send_part(stage, out, index, part):
        def one(step, carry):
            c = lax.rem(step + 1 + me_seq // parts, per_part)
            peer = head_of(part, c)
            send_seq(stage.at[peer], out, index, peer)
            return carry

        lax.fori_loop(0, per_part, one, 0)

    def seq_total(out, index):
        return pltpu.make_async_remote_copy(
            src_ref=out.at[pl.ds(1, heads - 1)],
            dst_ref=out.at[pl.ds(1, heads - 1)],
            send_sem=s_send.at[index],
            recv_sem=s_recv.at[index],
            device_id=(me_dp, lax.rem(me_seq + 1, heads)),
            device_id_type=MESH,
        )

    def dest_block(moved, kept, j):
        return jnp.where(tab[groups + 2, j] == 1, kept.astype(F32), moved.astype(F32))

    def pass_on(pool, here, stage, out, index, part):
        for j in range(LIVE):
            kept = here[tab[groups + 1, j]]
            kept = jnp.concatenate(
                [kept[:, h * HEAD:(h + 1) * HEAD] for h in [head_of(part, c) for c in range(per_part)]], axis=1
            )
            rows32[j * TOKENS:(j + 1) * TOKENS, : per_part * HEAD] = dest_block(
                pool[part][tab[groups, j]], kept, j
            )
        for c in range(per_part):
            stage[head_of(part, c)] = rows32[:, c * HEAD:(c + 1) * HEAD].astype(BF16)
        send_part(stage, out, index, part)

    loads[0].wait()
    pack(keys_here, keys_send, 0)
    pl.semaphore_wait(barrier, groups + heads - 2)
    for part in range(parts):
        if part > 0:
            pack(keys_here, keys_send, part)
        send_dp(keys_send.at[part], keys_pool[part], part)

    loads[3].wait()
    for j in range(LIVE):
        rows32[j * TOKENS:(j + 1) * TOKENS, :] = grad_buf[j].astype(F32)
    for h in range(heads):
        grad_stage[h] = rows32[:, h * HEAD:(h + 1) * HEAD].astype(BF16)
    for part in range(parts):
        send_part(grad_stage, grad_got, 3, part)

    loads[1].wait()
    loads[2].wait()
    for b in range(blocks):
        feat32[b * TOKENS:(b + 1) * TOKENS, :] = feat_buf[b].astype(F32)
    features = feat32[: blocks * TOKENS, :].astype(BF16)
    adapter = lax.dot_general(features, down_ref[...], nt, preferred_element_type=F32).astype(BF16)
    adapter32[: blocks * TOKENS, :] = jnp.concatenate([adapter, adapter], axis=1).astype(F32)
    up32[...] = jnp.dot(adapter, up_ref[...], preferred_element_type=F32)
    for b in range(blocks):
        query_here[b] = (query_here[b].astype(F32) + up32[b * TOKENS:(b + 1) * TOKENS, :]).astype(BF16)
        adapter_here[b] = adapter32[b * TOKENS:(b + 1) * TOKENS, :].astype(BF16)
    for i in range(slots):
        adapter_send[i] = adapter_here[slot_source(i)]
    send_dp(adapter_send, adapter_pool, 3 * parts)
    for part in range(parts):
        pack(query_here, query_send, part)
        send_dp(query_send.at[part], query_pool[part], parts + part)
    loads[4].wait()
    for part in range(parts):
        pack(values_here, values_send, part)
        send_dp(values_send.at[part], values_pool[part], 2 * parts + part)

    for i in range(slots):
        feat32[i * TOKENS:(i + 1) * TOKENS, :] = feat_buf[slot_source(i)].astype(F32)
    for k in range(groups - 1):
        feat_moving[k] = feat32[k * CAP * TOKENS:(k + 1) * CAP * TOKENS, :].astype(BF16)
    feat32[...] = jnp.zeros_like(feat32)
    pieces[...] = jnp.zeros_like(pieces)
    for j in range(LIVE):
        row = stay_row + j * TOKENS
        feat32[row:row + TOKENS, :] = feat_buf[tab[groups + 1, j]].astype(F32)

    def take_part(send, pool, here, stage, got, index, order, part):
        dp_part(send.at[part], pool[part], order * parts + part).wait_recv()
        pass_on(pool, here, stage, got, index, part)

    def position(first, rows):
        token = first + lax.broadcasted_iota(jnp.int32, (rows, HEAD), 0)
        part = (token * 52429) >> 22
        rest = token - part * ROWS
        owner = (me_seq - part) & (heads - 1)
        return (rest >> 2) * (TOKENS * heads) + owner * TOKENS + (rest & 3)

    live_count = jnp.sum((segments_ref[...] < 1).astype(jnp.int32), axis=1, keepdims=True)
    lane80 = lax.broadcasted_iota(jnp.int32, (ROWS, HEAD), 1)
    for part in range(parts):
        take_part(keys_send, keys_pool, keys_here, keys_stage, keys_got, 0, 0, part)
    dp_part(adapter_send, adapter_pool, 3 * parts).wait_recv()
    adapter32[...] = jnp.zeros_like(adapter32)
    for j in range(LIVE):
        adapter32[j * TOKENS:(j + 1) * TOKENS, :] = dest_block(
            adapter_pool[tab[groups, j]], adapter_here[tab[groups + 1, j]], j
        )
    lane = lax.broadcasted_iota(jnp.int32, (FOLD, HEAD), 1)
    adapter_stage[...] = jnp.where(
        lane < RANK, adapter32[0:FOLD, :], adapter32[FOLD:2 * FOLD, :]
    ).astype(BF16)

    def spread(k, carry):
        send_seq(adapter_stage, adapter_got, 4, lax.rem(me_seq + k, heads))
        return carry

    lax.fori_loop(0, heads, spread, 0)
    for k in range(heads):
        at = slice(k * ROWS, (k + 1) * ROWS)
        live = position(k * ROWS, ROWS) < live_count
        value_sum[at, HEAD:] = jnp.where(live, 1.0, 0.0).astype(BF16)
        value_neg[at, HEAD:] = jnp.where(lane80 < 3, -1.0, 0.0).astype(BF16)
    for part in range(parts):
        if part == parts // 2:
            seq_total(keys_got, 0).wait_recv()
            pltpu.make_async_copy(keys_stage.at[0], keys_got.at[0], own_sem.at[0]).wait()
            filler = keys_got[me_seq][0:1, :]
            for k in range(heads):
                at = slice(k * ROWS, (k + 1) * ROWS)
                live = position(k * ROWS, ROWS) < live_count
                rows = keys_got[k]
                key_max[at, :] = jnp.where(live, rows, filler)
                key_sum[at, :] = jnp.where(live, rows, zero)
        take_part(query_send, query_pool, query_here, query_stage, query_got, 2, 1, part)

    tops = []

    def score_tile(t):
        query = query_got[t * per_tile:(t + 1) * per_tile].reshape(tile, HEAD)
        top = None
        for c in range(0, total, step):
            part_scores = lax.dot_general(query, key_max[c:c + step, :], nt, preferred_element_type=F32)
            scores[:, c:c + step] = part_scores
            for b in range(0, step, HEAD):
                piece = part_scores[:, b:b + HEAD]
                top = piece if top is None or piece.shape != top.shape else jnp.maximum(top, piece)
        top = jnp.max(top if step % HEAD == 0 else scores[...], axis=1, keepdims=True)
        for c in range(0, total, step):
            probs[t * tile:(t + 1) * tile, c:c + step] = jnp.exp2(
                (scores[:, c:c + step] - top) * to_exp2
            ).astype(BF16)
        logs[t * tile:(t + 1) * tile, :] = jnp.broadcast_to(top * scaling, (tile, HEAD))

    def dp_copy(k, src, dst, index):
        return pltpu.make_async_remote_copy(
            src_ref=src, dst_ref=dst, send_sem=z_send.at[dp_base + index], recv_sem=z_recv.at[dp_base + index],
            device_id=(k, me_seq), device_id_type=MESH,
        )

    def seq_copy(k, src, dst, index):
        return pltpu.make_async_remote_copy(
            src_ref=src, dst_ref=dst, send_sem=s_send.at[seq_base + index], recv_sem=s_recv.at[seq_base + index],
            device_id=(me_dp, k), device_id_type=MESH,
        )

    def send_features(k, carry):
        dp_copy(lax.rem(me_dp + k, groups), feat_moving.at[k - 1], feat_recv.at[k - 1], 0).start()
        return carry

    for part in range(parts):
        take_part(values_send, values_pool, values_here, values_stage, values_got, 1, 2, part)
        if part == parts // tiles - 1:
            seq_total(query_got, 2).wait_recv()
            pltpu.make_async_copy(query_stage.at[0], query_got.at[0], own_sem.at[2]).wait()
        if part == parts - 1:
            lax.fori_loop(1, groups, send_features, 0)
        if (part + 1) % (parts // tiles) == 0:
            score_tile(part // (parts // tiles))

    up_copy.wait()
    up = up_head[...]
    nothing = jnp.zeros((RANK, HEAD), BF16)
    to_low = jnp.concatenate([up, nothing], axis=0)
    to_high = jnp.concatenate([nothing, up], axis=0)
    filling = jnp.zeros((2 * FOLD - ROWS, HEAD), BF16)
    lanes = lax.broadcasted_iota(jnp.int32, (tile, HEAD), 1)

    seq_total(grad_got, 3).wait_recv()
    pltpu.make_async_copy(grad_stage.at[0], grad_got.at[0], own_sem.at[3]).wait()
    seq_total(values_got, 1).wait_recv()
    pltpu.make_async_copy(values_stage.at[0], values_got.at[0], own_sem.at[1]).wait()
    for k in range(heads):
        at = slice(k * ROWS, (k + 1) * ROWS)
        value = jnp.where(position(k * ROWS, ROWS) < live_count, values_got[k], zero)
        value_sum[at, 0:HEAD] = value
        value_neg[at, 0:HEAD] = value

    state = [dict() for _ in range(tiles)]

    def attend_step(t, c):
        own = state[t]
        add = jnp.dot(
            probs[t * tile:(t + 1) * tile, c:c + step], value_sum[c:c + step, :], preferred_element_type=F32
        )
        own["sum"] = add if c == 0 else own["sum"] + add
        if c + step == total:
            norm = own["sum"][:, HEAD:]
            inverse = 1.0 / norm
            grad = grad_got[t * per_tile:(t + 1) * per_tile].reshape(tile, HEAD)
            delta = jnp.sum(grad.astype(F32) * own["sum"][:, :HEAD], axis=1, keepdims=True) * inverse
            high = delta.astype(BF16)
            middle = (delta - high.astype(F32)).astype(BF16)
            low = (delta - high.astype(F32) - middle.astype(F32)).astype(BF16)
            split = jnp.where(lanes == 0, high, jnp.where(lanes == 1, middle, jnp.where(lanes == 2, low, zero)))
            own["wide"] = jnp.concatenate([grad, split], axis=1)
            own["factor"] = inverse * scaling
            at = slice(t * tile, (t + 1) * tile)
            own["live"] = position(t * tile, tile) < live_count
            logs[at, :] = jnp.where(own["live"], logs[at, :] + jnp.log(norm), 0.0)

    def gradient_step(t, c):
        own = state[t]
        dprob = lax.dot_general(own["wide"], value_neg[c:c + step, :], nt, preferred_element_type=F32)
        dscore = (probs[t * tile:(t + 1) * tile, c:c + step].astype(F32) * dprob).astype(BF16)
        add = jnp.dot(dscore, key_sum[c:c + step, :], preferred_element_type=F32)
        own["grad"] = add if c == 0 else own["grad"] + add
        if c + step == total:
            result = jnp.where(own["live"], own["grad"] * own["factor"], 0.0).astype(BF16)
            dquery[t * tile:(t + 1) * tile, :] = result
            for i in range(per_tile):
                k = t * per_tile + i
                first_part = result[i * ROWS:i * ROWS + FOLD]
                second_part = jnp.concatenate([result[i * ROWS + FOLD:(i + 1) * ROWS], filling], axis=0)
                partial_send[k] = (
                    lax.dot_general(first_part, to_low, nt, preferred_element_type=F32)
                    + lax.dot_general(second_part, to_high, nt, preferred_element_type=F32)
                ).astype(BF16)
                if k > 0:
                    seq_copy(
                        lax.rem(me_seq + heads - k, heads), partial_send.at[k], partial_recv.at[k - 1], 0
                    ).start()

    for t in range(tiles + 1):
        for c in range(0, total, step):
            if t < tiles:
                attend_step(t, c)
            if t > 0:
                gradient_step(t - 1, c)

    seq_total(adapter_got, 4).wait_recv()
    pltpu.make_async_copy(adapter_stage, adapter_got.at[0], own_sem.at[4]).wait()
    up_total = jnp.zeros((RANK, HEAD), F32)
    for k in range(heads):
        first_part = dquery[k * ROWS:k * ROWS + FOLD, :]
        second_part = jnp.concatenate([dquery[k * ROWS + FOLD:(k + 1) * ROWS, :], filling], axis=0)
        folded = adapter_got[k]
        up_total = up_total + lax.dot_general(folded, first_part, tn, preferred_element_type=F32)[:RANK]
        up_total = up_total + lax.dot_general(folded, second_part, tn, preferred_element_type=F32)[RANK:]
    up_send[...] = jnp.zeros_like(up_send)
    for d in range(groups):
        up_send[d, 0:up_rows, :] = up_total[d * up_rows:(d + 1) * up_rows, :]

    def send_up(k, carry):
        peer = lax.rem(me_dp + k, groups)
        dp_copy(peer, up_send.at[peer], up_recv.at[k - 1], 1).start()
        return carry

    lax.fori_loop(1, groups, send_up, 0)

    def dp_total(like, index):
        return dp_copy(lax.rem(me_dp + 1, groups), like, like, index)

    dp_total(feat_recv, 0).wait_recv()
    for k in range(groups - 1):
        feat32[k * CAP * TOKENS:(k + 1) * CAP * TOKENS, :] = feat_recv[k].astype(F32)
    feat_turned[...] = feat32[...].T.astype(BF16)

    partial_total = seq_copy(lax.rem(me_seq + 1, heads), partial_send.at[pl.ds(1, heads - 1)], partial_recv, 0)
    partial_total.wait_recv()
    folded = partial_send[0].astype(F32)
    for k in range(heads - 1):
        folded = folded + partial_recv[k].astype(F32)
    turned = pltpu.roll(folded, RANK, 1)
    for j in range(LIVE):
        row = j * TOKENS
        half = folded if row < FOLD else turned
        row = row if row < FOLD else row - FOLD
        blocks32[j] = half[row:row + TOKENS, :]
    blocks32[LIVE] = jnp.zeros((TOKENS, HEAD), F32)
    for k in range(1, groups):
        origin = lax.rem(me_dp + groups - k, groups)
        for r in range(CAP):
            row = ((k - 1) * CAP + r) * TOKENS
            pieces[row:row + TOKENS, :] = blocks32[tab[origin, CAP + r]]
    for j in range(LIVE):
        stays = tab[groups + 2, j].astype(F32)
        row = stay_row + j * TOKENS
        pieces[row:row + TOKENS, :] = blocks32[j] * stays
    own_lane = lax.broadcasted_iota(jnp.int32, pieces.shape, 1)
    grads = pieces[...]
    doubled = jnp.where(own_lane < RANK, grads, pltpu.roll(grads, RANK, 1)).astype(BF16)
    down = jnp.dot(feat_turned[...], doubled, preferred_element_type=F32)
    fold_lane = lax.broadcasted_iota(jnp.int32, (FOLD, HEAD), 1)
    for h in range(heads):
        first = down[h * ROWS:h * ROWS + FOLD, :]
        second = jnp.concatenate(
            [down[h * ROWS + FOLD:(h + 1) * ROWS, :], jnp.zeros((2 * FOLD - ROWS, HEAD), F32)], axis=0
        )
        down_send[h % rows_x, h // rows_x] = jnp.where(fold_lane < RANK, first, second).astype(BF16)
    me_x, me_y = lax.rem(me_seq, rows_x), me_seq // rows_x

    def send_down_x(k, carry):
        peer = lax.rem(me_x + k, rows_x)
        seq_copy(me_y * rows_x + peer, down_send.at[peer], down_x.at[k - 1], 1).start()
        return carry

    lax.fori_loop(1, rows_x, send_down_x, 0)

    dp_total(up_recv, 1).wait_recv()
    up_sum = up_send[me_dp]
    for k in range(groups - 1):
        up_sum = up_sum + up_recv[k]
    total_send[...] = up_sum * scale

    def send_total(k, carry):
        dp_copy(lax.rem(me_dp + k, groups), total_send, total_recv.at[k - 1], 2).start()
        return carry

    lax.fori_loop(1, groups, send_total, 0)
    gathered = jnp.zeros((ROWS, HEAD), F32)
    row = lax.broadcasted_iota(jnp.int32, (ROWS, HEAD), 0)
    for k in range(heads):
        owner = (me_seq - k) & (heads - 1)
        column = owner * TOKENS + (row & 3)
        gathered = gathered + jnp.where(lane80 == column, logs[k * ROWS:(k + 1) * ROWS, :], 0.0)
    pick = lax.broadcasted_iota(jnp.int32, log_ref.shape[:1] + (ROWS,), 1) >> 2
    pick = (pick == lax.broadcasted_iota(jnp.int32, pick.shape, 0)).astype(F32)
    log_ref[...] = jnp.dot(pick, gathered, preferred_element_type=F32, precision=lax.Precision.HIGHEST)
    down_x_total = seq_copy(lax.rem(me_seq + 1, heads), down_x, down_x, 1)
    down_x_total.wait_recv()
    for row in range(rows_y):
        share = down_send[me_x, row].astype(F32)
        for k in range(rows_x - 1):
            share = share + down_x[k, row].astype(F32)
        down_row[row] = share.astype(BF16)

    def send_down_y(k, carry):
        peer = lax.rem(me_y + k, rows_y)
        seq_copy(peer * rows_x + me_x, down_row.at[peer], down_y.at[k - 1], 2).start()
        return carry

    lax.fori_loop(1, rows_y, send_down_y, 0)
    dp_total(total_recv, 2).wait_recv()
    whole32[me_dp] = total_send[...]
    for k in range(1, groups):
        whole32[lax.rem(me_dp + groups - k, groups)] = total_recv[k - 1]
    for d in range(groups):
        up_out[d * up_rows:(d + 1) * up_rows, :] = whole32[d, 0:up_rows, :]

    down_y_total = seq_copy(lax.rem(me_seq + 1, heads), down_y, down_y, 2)
    down_y_total.wait_recv()
    share = down_row[me_y].astype(F32)
    for k in range(rows_y - 1):
        share = share + down_y[k].astype(F32)
    share_recv[0] = share.astype(BF16)

    def send_share(k, carry):
        dp_copy(lax.rem(me_dp + k, groups), share_recv.at[0], share_recv.at[k], 3).start()
        return carry

    lax.fori_loop(1, groups, send_share, 0)
    share_total = dp_total(share_recv.at[pl.ds(1, groups - 1)], 3)
    share_total.wait_recv()
    share = jnp.zeros((FOLD, HEAD), F32)
    for d in range(groups):
        share = share + share_recv[lax.rem(me_dp + groups - d, groups)].astype(F32)
    share = share * scale
    turned = pltpu.roll(share, RANK, 1)
    whole = jnp.concatenate(
        [share, turned[:ROWS - FOLD], jnp.zeros((HEAD - ROWS, HEAD), F32)], axis=0
    )
    down_out[...] = whole.T[:RANK, :ROWS]

    dp_total(feat_recv, 0).wait_send()
    dp_total(up_recv, 1).wait_send()
    dp_total(total_recv, 2).wait_send()
    share_total.wait_send()
    partial_total.wait_send()
    down_x_total.wait_send()
    down_y_total.wait_send()
    for part in range(parts):
        dp_part(keys_send.at[part], keys_pool[part], part).wait_send()
        dp_part(query_send.at[part], query_pool[part], parts + part).wait_send()
        dp_part(values_send.at[part], values_pool[part], 2 * parts + part).wait_send()
    dp_part(adapter_send, adapter_pool, 3 * parts).wait_send()
    for index, got in enumerate((keys_got, values_got, query_got, grad_got, adapter_got)):
        seq_total(got, index).wait_send()


def whole(tables, segments, down_t, up, keys, values, base, grads, features, scale, groups, heads):
    blocks = keys.shape[0]
    slots = (groups - 1) * CAP
    width = heads * HEAD
    total = heads * ROWS
    parts = min(PARTS, heads)
    inputs = features.shape[2]
    vmem = pl.BlockSpec(memory_space=pltpu.VMEM)
    hbm = pl.BlockSpec(memory_space=pl.ANY)
    up_tile = max(8, RANK // groups)
    feat_rows = -(-max(slots, blocks) * TOKENS // HEAD) * HEAD + HEAD
    rows_x, rows_y = seq_shape(heads)

    def array(*shape, dtype=BF16):
        return pltpu.VMEM(shape, dtype)

    def numbers(*shape):
        return pltpu.VMEM(shape, F32)

    arriving = array(slots, TOKENS, width // parts)
    moving = array(parts, slots, TOKENS, width // parts)
    here = array(blocks, TOKENS, width)
    chunks = array(heads, ROWS, HEAD)
    folded = array(heads, FOLD, HEAD)
    received = array(heads - 1, FOLD, HEAD)
    return pl.pallas_call(
        functools.partial(whole_kernel, groups, heads, parts, scale),
        out_shape=(
            jax.ShapeDtypeStruct((RANK, ROWS), F32),
            jax.ShapeDtypeStruct((RANK, HEAD), F32),
            jax.ShapeDtypeStruct((blocks, HEAD), F32),
        ),
        in_specs=[pl.BlockSpec(memory_space=pltpu.SMEM)] + [vmem] * 3 + [hbm] * 5,
        out_specs=[vmem] * 3,
        scratch_shapes=[arriving] * (3 * parts) + [
            array(slots, TOKENS, HEAD),
            here, here, here, array(blocks, TOKENS, HEAD), here, array(blocks, TOKENS, inputs),
            moving, moving, moving, array(slots, TOKENS, HEAD),
            chunks, chunks, chunks, chunks, array(FOLD, HEAD),
            numbers(ROWS, width),
            numbers(feat_rows, inputs),
            numbers(blocks * TOKENS, width),
            numbers(max(blocks * TOKENS, 2 * FOLD), HEAD),
            chunks, chunks, chunks, chunks, folded,
            array(groups - 1, CAP * TOKENS, inputs), array(inputs, feat_rows),
            array(total, HEAD), array(total, HEAD), array(total, 2 * HEAD), array(total, 2 * HEAD),
            numbers(total // min(4, heads), total), array(total, total), array(total, HEAD), numbers(total, HEAD),
            array(RANK, HEAD),
            array(groups - 1, CAP * TOKENS, inputs),
            folded, received,
            numbers(LIVE + 1, TOKENS, HEAD), numbers(feat_rows, HEAD),
            array(rows_x, rows_y, FOLD, HEAD), array(rows_x - 1, rows_y, FOLD, HEAD),
            array(rows_y, FOLD, HEAD), array(rows_y - 1, FOLD, HEAD),
            numbers(groups, up_tile, HEAD), numbers(groups - 1, up_tile, HEAD),
            numbers(up_tile, HEAD), numbers(groups - 1, up_tile, HEAD), numbers(groups, up_tile, HEAD),
            array(groups, FOLD, HEAD),
            pltpu.SemaphoreType.DMA,
            pltpu.SemaphoreType.DMA((5,)),
            pltpu.SemaphoreType.DMA((5,)),
            pltpu.SemaphoreType.DMA((3 * parts + 5,)),
            pltpu.SemaphoreType.DMA((3 * parts + 5,)),
            pltpu.SemaphoreType.DMA((8,)),
            pltpu.SemaphoreType.DMA((8,)),
        ],
        compiler_params=pltpu.CompilerParams(
            collective_id=1, has_side_effects=True, vmem_limit_bytes=VMEM_LIMIT
        ),
        name="whole",
    )(tables, segments, down_t, up, keys, values, base, grads, features)


def per_device(
    features, frozen_query_weight, source_keys, source_values, output_gradient,
    adapter_down_weight, adapter_up_weight, source_block_plan, segments,
):
    groups = lax.axis_size("dp")
    heads = lax.axis_size("seq")
    length = segments.shape[1]
    tables = block_tables(source_block_plan, groups)
    scale = 4.0 / math.sqrt(groups * length)
    down, up, logs = whole(
        tables, segments, adapter_down_weight.T, adapter_up_weight, source_keys[0], source_values[0],
        frozen_query_weight[0], output_gradient[0], features[0], scale, groups, heads,
    )
    log_norm = logs[:, : TOKENS * heads].reshape(1, 1, length)
    return (down.T, up, log_norm)


def solution(mesh):
    in_specs = (
        P("dp", None, "seq", None),
        P("dp", None, "seq", None),
        P("dp", None, "seq", None),
        P("dp", None, "seq", None),
        P("dp", None, "seq", None),
        P(),
        P(),
        P(),
        P("dp", None),
    )
    out_specs = (P("seq", None), P(None, "seq"), P("dp", "seq", None))
    return jax.shard_map(
        per_device, mesh=mesh, in_specs=in_specs, out_specs=out_specs, check_vma=False
    )
```
